512 devices in a mesh: wide: 64 (over y, z), narrow: 8 (over x, core).
Axes of the slice: x: 4, y: 8, z: 8, core: 2. Of those that a mesh axis runs over, the one named last changes fastest.
Arguments:
- pressure: float32 [512, 512, 512], P('wide', 'narrow'), may hold values from -6 to 6
Outputs:
- detail_one: float32 [7, 256, 256, 256], P(None, 'wide', 'narrow')
- detail_two: float32 [7, 128, 128, 128], P(None, 'wide', 'narrow')
- detail_three: float32 [7, 64, 64, 64], P(None, 'wide', 'narrow')
- bands_four: float32 [8, 32, 32, 32], P(None, None, 'narrow')
The draws below stay inside these ranges and needn't reach their ends.
All inputs are finite; a program needn't handle non-finite values.
Results may differ from the reference program's by a relative error of at most 0.00016.
Values sent between devices are 32-bit elements; how exact they have to be, the bound alone decides.
A program may use at most 64 MiB of HBM per device.

```python
import jax
import jax.numpy as jnp
from jax import lax

COLS = 512
LEVELS = 4
NZ = 512
NY = 512


def block_scale(key, extent, pieces, least, largest):
    gain, own = 1.0, jax.random.fold_in(key, 6)
    for axis_at, blocks in pieces:
        heights = jnp.exp(jax.random.uniform(jax.random.fold_in(own, axis_at), (blocks,), jnp.float32, least / len(pieces), largest / len(pieces)))
        gain = gain * jnp.repeat(heights, extent[axis_at] // blocks).reshape([-1 if axis == axis_at else 1 for axis in range(len(extent))])
    return gain


def gaussian(stream_key, dims, spread, bound, split=(), kind=jnp.bfloat16):
    result = jax.random.normal(stream_key, dims, jnp.float32) * spread
    if len(split) > 0:
        result = block_scale(stream_key, dims, split, -0.22, 0.18) * result
    return jnp.clip(result, min=-bound, max=bound).astype(kind)


def setup_inputs(seed: int = 0) -> dict:
    key_list = jax.random.split(jax.random.key(seed), 2)
    pressure = gaussian(key_list[0], (NZ, NY, COLS), 1.0, 6.0, ((0, 64), (1, 8)), jnp.float32)
    return {"pressure": pressure}


LIFT_ALPHA = -1.586134342
LIFT_BETA = -0.05298011854
LIFT_GAMMA = 0.8829110762
LIFT_DELTA = 0.4435068522
LIFT_ZETA = 1.149604398
LIFT_INVERSE = 1.0 / 1.149604398


def lift_line(volume, along):
    length = volume.shape[along]
    half = length // 2
    even_part = lax.slice_in_dim(volume, 0, length, 2, along)
    odd_part = lax.slice_in_dim(volume, 1, length, 2, along)

    def next_even(source):
        return jnp.concatenate([lax.slice_in_dim(source, 1, half, 1, along), lax.slice_in_dim(source, half - 1, half, 1, along)], along)

    def prev_odd(source):
        return jnp.concatenate([lax.slice_in_dim(source, 0, 1, 1, along), lax.slice_in_dim(source, 0, half - 1, 1, along)], along)

    odd_part = odd_part + LIFT_ALPHA * (even_part + next_even(even_part))
    even_part = even_part + LIFT_BETA * (prev_odd(odd_part) + odd_part)
    odd_part = odd_part + LIFT_GAMMA * (even_part + next_even(even_part))
    even_part = even_part + LIFT_DELTA * (prev_odd(odd_part) + odd_part)
    return jnp.stack([even_part * LIFT_ZETA, odd_part * LIFT_INVERSE], 0)


def one_level(volume):
    x_pair = lift_line(volume, 2)
    y_pair = lift_line(x_pair, 2)
    z_pair = lift_line(y_pair, 2)
    return z_pair.reshape((8,) + z_pair.shape[3:])


def reference(pressure):
    volume = pressure
    details = []
    band_set = None
    for _ in range(LEVELS):
        band_set = one_level(volume)
        details.append(band_set[1:])
        volume = band_set[0]
    return details[0], details[1], details[2], band_set
```

```python
import jax
import jax.numpy as jnp
import ml_dtypes
import numpy as np
from jax import lax
from jax.experimental import pallas as pl
from jax.experimental.pallas import tpu as pltpu
from jax.sharding import PartitionSpec as P

MESH = pl.DeviceIdType.MESH
F32, BF16 = jnp.float32, jnp.bfloat16

LA = -1.586134342
LB = -0.05298011854
LG = 0.8829110762
LD = 0.4435068522
LZ = 1.149604398
LI = 1.0 / 1.149604398


def lift_matrix(n):
    v = np.eye(n)
    s, d = v[0::2].copy(), v[1::2].copy()

    def nxt(q):
        return np.concatenate([q[1:], q[-1:]])

    def prv(q):
        return np.concatenate([q[:1], q[:-1]])

    d = d + LA * (s + nxt(s))
    s = s + LB * (prv(d) + d)
    d = d + LG * (s + nxt(s))
    s = s + LD * (prv(d) + d)
    return np.concatenate([s * LZ, d * LI])


def chain():
    out, low = {}, np.eye(512)
    for k in (1, 2, 3, 4):
        out[k] = lift_matrix(1024 >> k) @ low
        low = out[k][: 512 >> k]
    return out


CH = chain()
L64 = lift_matrix(64)
H_LOW = [float(L64[16, 32 + k]) for k in range(5)]
H_HIGH = [float(L64[48, 33 + k]) for k in range(4)]


def two(a):
    hi = a.astype(ml_dtypes.bfloat16)
    return hi, (a - hi.astype(np.float64)).astype(ml_dtypes.bfloat16)


def stack_rhs(a):
    hi, lo = two(a)
    return np.concatenate([hi, hi, lo], axis=0)


def stack_lhs(a):
    hi, lo = two(a)
    return np.concatenate([hi, hi, lo], axis=-1)


def y_rows(k, n):
    half, own = 512 >> k, 64 >> k
    return list(range(n * own, (n + 1) * own)) + list(range(half + n * own, half + (n + 1) * own))


def y_block(k, to, cells, rows):
    if not 0 <= to < 8:
        return np.zeros((len(rows), 64))
    return CH[k][[y_rows(k, to)[r] for r in rows]][:, 64 * cells : 64 * cells + 64]


def y_table(k, n):
    own = 64 >> k
    up = list(range(4)) + list(range(own, own + 4))
    down = list(range(2 * own - 4, 2 * own)) + list(range(own - 4, own))
    for to, rows in ((n + 1, up), (n - 1, down)):
        if 0 <= to < 8:
            rest = [r for r in range(2 * own) if r not in rows]
            assert not rest or abs(y_block(k, to, n, rest)).max() < 1e-15
    return np.concatenate(
        [y_block(k, n, n, list(range(2 * own))), y_block(k, n + 1, n, up), y_block(k, n - 1, n, down)]
    )


def y4_table(n):
    rows = np.concatenate([y_block(4, to, n, list(range(8))) for to in (n, n + 1, n - 1)])
    return np.einsum("ry,pq->rpqy", rows, np.eye(8)).reshape(24 * 8, 512)


def tables():
    x4 = CH[4].T
    t = {}
    t["x34"] = stack_rhs(np.concatenate([CH[3].T, x4, x4], axis=1))
    t["x2"] = stack_rhs(CH[2].T)
    t["x1"] = stack_rhs(CH[1].T)
    t["y4"] = np.stack([stack_lhs(y4_table(n)) for n in (0, 3, 7)])
    t["y3"] = np.stack([stack_lhs(y_table(3, n)) for n in range(8)])
    t["y2"] = np.stack([stack_lhs(y_table(2, n)) for n in range(8)])
    low3 = CH[3][:64]
    ca = np.zeros((8, 16, 64))
    fin = np.zeros((64, 128))
    for y in range(8):
        for s in range(15):
            w = 8 * y - 3 + s
            if 0 <= w < 64:
                ca[y, s] = low3[w, 64 * y : 64 * y + 64]
                fin[:, 16 * y + s] = L64[:, w]
        for w in range(64):
            if not 8 * y - 3 <= w <= 8 * y + 11:
                assert abs(low3[w, 64 * y : 64 * y + 64]).max() < 1e-15
    t["ca"] = np.stack([stack_lhs(ca[y]) for y in range(8)])
    t["fin"] = stack_lhs(fin)
    c3 = np.zeros((64, 8, 2, 8), np.float32)
    for w in range(64):
        for i in range(8):
            to = w + i - 3
            if 0 <= to < 64:
                c3[w, i, 0] = CH[3][to, 8 * w : 8 * w + 8]
                c3[w, i, 1] = CH[3][64 + to, 8 * w : 8 * w + 8]
    t["c3"] = c3.reshape(64, 1, 128)
    return t


TAB = tables()
NAMES = ("x34", "y4", "x2", "y3", "y2", "x1", "ca", "fin", "c3")


def halves(x):
    hi = x.astype(BF16)
    return hi, (x - hi.astype(F32)).astype(BF16)


def data_rhs(x):
    hi, lo = halves(x)
    return jnp.concatenate([hi, lo, hi], axis=0)


def dot(a, b):
    return jnp.dot(a, b, preferred_element_type=F32)


def z_states(planes):
    s0, d0, s1 = planes[0], planes[1], planes[2]
    p1 = s0 + LB * (d0 + LA * (s0 + s1))
    sl, dl = planes[-2], planes[-1]
    u1 = dl + LA * sl
    u2 = sl + LB * (planes[-3] + LA * (planes[-4] + sl))
    return (s0, p1), (u1, u2)


def z_lift(planes, p0, p1, u1, u2, first, last, need_high):
    s, d = planes[0::2], planes[1::2]
    m = len(s)
    n0 = jnp.where(last, s[-1], p0)
    d = [d[i] + LA * (s[i] + (s[i + 1] if i + 1 < m else n0)) for i in range(m)]
    before = jnp.where(first, d[0], u1 + LA * s[0])
    s_old = s
    s = [s[i] + LB * ((d[i - 1] if i else before) + d[i]) for i in range(m)]
    n1 = jnp.where(last, s[-1], p1 + LB * d[-1])
    d1 = d
    d = [d[i] + LG * (s[i] + (s[i + 1] if i + 1 < m else n1)) for i in range(m)]
    before2 = jnp.where(first, d[0], before + LG * (u2 + LB * before + s[0]))
    del s_old, d1
    low = [(s[i] + LD * ((d[i - 1] if i else before2) + d[i])) * LZ for i in range(m)]
    return low, [x * LI for x in d] if need_high else None


def main_kernel(v_hbm, x34_h, y4_h, x2_h, y3_h, y2_h, x1_h, ca_h, fin_h, c3_h,
                d1_o, d2_o, d3_o, f_o,
                v, vc, x34, y4, x2, y3, y2, x1, ca, fin, c3,
                so4, ri4, so3, ri3, so2, ri2, t3, t2, ga, gb, st1, zh1, e1, st2, zh2, t2b, st2b, zh2b, s3, r3,
                lsem, ss, rs):
    w, n = lax.axis_index("wide"), lax.axis_index("narrow")
    y, z = w // 8, w % 8
    wfirst, wlast = w == 0, w == 63
    nfirst, nlast = n == 0, n == 7
    n_up, n_dn = (n + 1) % 8, (n + 7) % 8
    w_up, w_dn = (w + 1) % 64, (w + 63) % 64

    loads = [pltpu.make_async_copy(v_hbm, v, lsem.at[0])]
    variant = jnp.minimum(n, 1) + n // 7
    for i, (src, dst) in enumerate(
        (
            (x34_h, x34), (y4_h.at[variant], y4), (x2_h, x2), (y3_h.at[n], y3), (y2_h.at[n], y2),
            (x1_h, x1), (ca_h.at[y], ca), (fin_h, fin), (c3_h.at[w], c3),
        )
    ):
        loads.append(pltpu.make_async_copy(src, dst, lsem.at[1 + i]))
    for c in loads:
        c.start()
    l_v, l_x34, l_y4, l_x2, l_y3, l_y2, l_x1, l_ca, l_fin, l_c3 = loads

    barrier = pltpu.get_barrier_semaphore()
    peers = [(w, n_up), (w, n_dn)]
    peers += [((w + 64 + d) % 64, n) for d in (1, -1, 2, -2, 3, -3, 4, -4)]
    peers += [(y * 8 + (z + d) % 8, n) for d in range(1, 8)]
    peers += [(((y + d) % 8) * 8 + z, n) for d in range(1, 8)]
    for p in peers:
        pl.semaphore_signal(barrier, inc=1, device_id=p, device_id_type=MESH)

    count = [0]
    started = []

    def send(src, dst, to):
        k = count[0]
        count[0] += 1
        c = pltpu.make_async_remote_copy(
            src_ref=src, dst_ref=dst, send_sem=ss.at[k], recv_sem=rs.at[k], device_id=to, device_id_type=MESH
        )
        c.start()
        started.append(c)
        return c

    l_v.wait()
    hi, lo = halves(v[...].reshape(512, 512))
    vc[:, 0:512] = hi
    vc[:, 512:1024] = lo
    vc[:, 1024:1536] = hi
    l_x34.wait()
    xa = dot(vc[...], x34[...])
    l_y4.wait()
    o4 = dot(y4[...], data_rhs(xa[:, 128:256])).reshape(24, 8, 128)
    lane_low = lax.broadcasted_iota(jnp.int32, (8, 128), 1) < 64

    def packed(base):
        return [jnp.where(lane_low, o4[base + r], o4[base + 4 + r]) for r in range(4)]

    own4, up4, dn4 = packed(0), packed(8), packed(16)
    for r in range(4):
        so4[0, r] = up4[r]
        so4[1, r] = dn4[r]

    pl.semaphore_wait(barrier, len(peers))
    a4 = [send(so4.at[0], ri4.at[0], (w, n_up)), send(so4.at[1], ri4.at[1], (w, n_dn))]

    (q0, q1), (q2, q3) = z_states([v[i] for i in range(8)])
    st1[0], st1[1], st1[2], st1[3] = q0, q1, q2, q3
    a1 = [
        send(st1.at[pl.ds(0, 2)], zh1.at[pl.ds(0, 2)], (w_dn, n)),
        send(st1.at[pl.ds(2, 2)], zh1.at[pl.ds(2, 2)], (w_up, n)),
    ]

    l_y3.wait()
    for p in range(8):
        o = dot(y3[...], data_rhs(xa[64 * p : 64 * p + 64, 0:128]))
        t3[p] = o[0:16]
        so3[0, p] = o[16:24]
        so3[1, p] = o[24:32]
    a3 = [send(so3.at[0], ri3.at[0], (w, n_up)), send(so3.at[1], ri3.at[1], (w, n_dn))]
    l_x2.wait()
    l_y2.wait()
    xb = dot(vc[...], x2[...])
    for p in range(8):
        o = dot(y2[...], data_rhs(xb[64 * p : 64 * p + 64]))
        t2[p] = o[0:32]
        so2[0, p] = o[32:40]
        so2[1, p] = o[40:48]
    a2 = [send(so2.at[0], ri2.at[0], (w, n_up)), send(so2.at[1], ri2.at[1], (w, n_dn))]

    for c in a4:
        c.wait_recv()
    here = pl.ds(pl.multiple_of(z * 8, 8), 8)
    for r in range(4):
        add = jnp.where(nfirst, 0.0, ri4[0, r]) + jnp.where(nlast, 0.0, ri4[1, r])
        ga[r, here, :] = own4[r] + add
    ga_sends = [
        send(ga.at[:, here, :], ga.at[:, here, :], (y * 8 + (z + d) % 8, n)) for d in (4, 3, 5, 2, 6, 1, 7)
    ]

    def add_parts(t, ri, own):
        width = t.shape[-1]
        sub_low = lax.broadcasted_iota(jnp.int32, (8, width), 0) < 4
        for p in range(8):
            up = jnp.where(nfirst, 0.0, ri[0, p])
            dn = jnp.where(nlast, 0.0, ri[1, p])
            up_r, dn_r = pltpu.roll(up, 4, 0), pltpu.roll(dn, 4, 0)
            t[p, 0:8] = t[p, 0:8] + jnp.where(sub_low, up, 0.0)
            t[p, own : own + 8] = t[p, own : own + 8] + jnp.where(sub_low, up_r, 0.0)
            t[p, own - 8 : own] = t[p, own - 8 : own] + jnp.where(sub_low, 0.0, dn)
            t[p, 2 * own - 8 : 2 * own] = t[p, 2 * own - 8 : 2 * own] + jnp.where(sub_low, 0.0, dn_r)

    for c in a2:
        c.wait_recv()
    add_parts(t2, ri2, 16)
    (q0, q1), (q2, q3) = z_states([t2[i] for i in range(8)])
    st2[0], st2[1], st2[2], st2[3] = q0, q1, q2, q3
    b2 = [
        send(st2.at[pl.ds(0, 2)], zh2.at[pl.ds(0, 2)], (w_dn, n)),
        send(st2.at[pl.ds(2, 2)], zh2.at[pl.ds(2, 2)], (w_up, n)),
    ]

    for c in a3:
        c.wait_recv()
    add_parts(t3, ri3, 8)
    l_c3.wait()
    planes3 = [t3[p] for p in range(8)]
    b3 = []
    for i in (7, 6, 5, 4, 2, 1, 0, 3):
        for j in range(2):
            acc = planes3[0] * c3[0, i * 16 + j * 8]
            for p in range(1, 8):
                acc = acc + planes3[p] * c3[0, i * 16 + j * 8 + p]
            s3[i, j] = acc
        if i != 3:
            b3.append(send(s3.at[i], r3.at[i], ((w + 64 + i - 3) % 64, n)))

    l_ca.wait()
    for c in ga_sends:
        c.wait_recv()
    cat = jnp.concatenate([ga[r] for r in range(4)], axis=1)
    part = dot(ca[...], data_rhs(cat))
    for r in range(4):
        gb[y, r] = part[:, 128 * r : 128 * r + 128]
    gb_sends = [send(gb.at[y], gb.at[y], (((y + d) % 8) * 8 + z, n)) for d in (4, 3, 5, 2, 6, 1, 7)]

    for c in b2:
        c.wait_recv()
    low, _ = z_lift([t2[i] for i in range(8)], zh2[0], zh2[1], zh2[2], zh2[3], wfirst, wlast, False)
    (q0, q1), (q2, q3) = z_states(low)
    for i in range(4):
        t2b[i] = low[i]
    st2b[0], st2b[1], st2b[2], st2b[3] = q0, q1, q2, q3
    c2 = [
        send(st2b.at[pl.ds(0, 2)], zh2b.at[pl.ds(0, 2)], (w_dn, n)),
        send(st2b.at[pl.ds(2, 2)], zh2b.at[pl.ds(2, 2)], (w_up, n)),
    ]

    for c in a1:
        c.wait_recv()
    for q in range(8):
        rows = slice(8 * q, 8 * q + 8)
        low, high = z_lift(
            [v[i, rows] for i in range(8)], zh1[0, rows], zh1[1, rows], zh1[2, rows], zh1[3, rows], wfirst, wlast, True
        )
        for i in range(4):
            v[i, rows] = low[i]
            v[4 + i, rows] = high[i]
    hi, lo = halves(v[...].reshape(512, 512))
    vc[:, 0:512] = hi
    vc[:, 512:1024] = lo
    vc[:, 1024:1536] = hi
    l_x1.wait()
    for h in range(2):
        o = dot(vc[...], x1[:, 256 * h : 256 * h + 256]).reshape(8, 64, 256)
        for q in range(2):
            e1[2 * h + q, :, 8:72, :] = o[:, :, 128 * q : 128 * q + 128]
    c1 = [
        send(e1.at[:, :, pl.ds(64, 8), :], e1.at[:, :, pl.ds(0, 8), :], (w, n_up)),
        send(e1.at[:, :, pl.ds(8, 8), :], e1.at[:, :, pl.ds(72, 8), :], (w, n_dn)),
    ]

    for c in b3:
        c.wait_recv()
    for j in range(2):
        acc = s3[3, j]
        for i in range(8):
            if i != 3:
                src = w - (i - 3)
                acc = acc + jnp.where((src >= 0) & (src < 64), r3[i, j], 0.0)
        for b in range(4):
            band = 4 * j + b
            if band:
                rows = slice(8 * (b // 2), 8 * (b // 2) + 8)
                cols = slice(64 * (b % 2), 64 * (b % 2) + 64)
                d3_o[band - 1, 0] = acc[rows, cols]

    for c in c2:
        c.wait_recv()
    low, high = z_lift([t2b[i] for i in range(4)], zh2b[0], zh2b[1], zh2b[2], zh2b[3], wfirst, wlast, True)
    for band in range(1, 8):
        src = high if band >= 4 else low
        by, bx = (band // 2) % 2, band % 2
        for i in range(2):
            d2_o[band - 1, i] = src[i][16 * by : 16 * by + 16, 128 * bx : 128 * bx + 128]

    for c in c1:
        c.wait_recv()

    @pl.when(nfirst)
    def _():
        for k in range(1, 5):
            e1[:, :, 8 - k : 9 - k, :] = e1[:, :, 8 + k : 9 + k, :]

    @pl.when(nlast)
    def _():
        for k in range(1, 5):
            e1[:, :, 71 + k : 72 + k, :] = e1[:, :, 71 - k : 72 - k, :]

    def tap(c, i, off):
        return e1[c, i, pl.ds(8 + off, 32, stride=2), :]

    for i in range(8):
        bz, zz = i // 4, i % 4
        for c in range(4):
            bx, cols = c // 2, slice(128 * (c % 2), 128 * (c % 2) + 128)
            if bz or bx:
                low = H_LOW[0] * tap(c, i, 0)
                for k in range(1, 5):
                    low = low + H_LOW[k] * (tap(c, i, -k) + tap(c, i, k))
                d1_o[4 * bz + bx - 1, zz, :, cols] = low
            high = H_HIGH[0] * tap(c, i, 1)
            for k in range(1, 4):
                high = high + H_HIGH[k] * (tap(c, i, 1 - k) + tap(c, i, 1 + k))
            d1_o[4 * bz + 2 + bx - 1, zz, :, cols] = high

    l_fin.wait()
    for c in gb_sends:
        c.wait_recv()
    cat = jnp.concatenate([gb[:, r].reshape(128, 128) for r in range(4)], axis=1)
    f_o[...] = dot(fin[...], data_rhs(cat))

    for c in started:
        c.wait_send()


def write_kernel(d1, d2, d3, f, o1, o2, o3, o4, buf, sem):
    copies = [pltpu.make_async_copy(a, b, sem.at[i]) for i, (a, b) in enumerate(((d1, o1), (d2, o2), (d3, o3)))]
    for c in copies:
        c.start()
    for bz in range(2):
        for r in range(4):
            tile = f[32 * bz : 32 * bz + 32, 128 * r : 128 * r + 128]
            for b in range(4):
                buf[4 * bz + b, :, r, :] = tile[:, 32 * b : 32 * b + 32]
    last = pltpu.make_async_copy(buf, o4, sem.at[3])
    last.start()
    for c in copies + [last]:
        c.wait()


VM, ANY = pl.BlockSpec(memory_space=pltpu.VMEM), pl.BlockSpec(memory_space=pl.ANY)
OUTS = ((7, 4, 32, 256), (7, 2, 16, 128), (7, 1, 8, 64), (8, 32, 4, 32))


def per_device(pressure):
    tabs = [jnp.asarray(TAB[k]) for k in NAMES]
    vm = lambda *s: pltpu.VMEM(s, F32)
    vb = lambda *s: pltpu.VMEM(s, BF16)
    sems = 64
    mids = OUTS[:3] + ((64, 512),)
    mid = pl.pallas_call(
        main_kernel,
        out_shape=[jax.ShapeDtypeStruct(s, F32) for s in mids],
        in_specs=[ANY] * 10,
        out_specs=[VM] * 4,
        scratch_shapes=[
            vm(8, 64, 512), vb(512, 1536),
            vb(1536, 256), vb(192, 1536), vb(1536, 256), vb(32, 192), vb(48, 192), vb(1536, 512),
            vb(16, 192), vb(64, 384), pltpu.SMEM((1, 128), F32),
            vm(2, 4, 8, 128), vm(2, 4, 8, 128), vm(2, 8, 8, 128), vm(2, 8, 8, 128), vm(2, 8, 8, 256), vm(2, 8, 8, 256),
            vm(8, 16, 128), vm(8, 32, 256), vm(4, 64, 128), vm(8, 4, 16, 128),
            vm(4, 64, 512), vm(4, 64, 512), vm(4, 8, 80, 128),
            vm(4, 32, 256), vm(4, 32, 256), vm(4, 32, 256), vm(4, 32, 256), vm(4, 32, 256),
            vm(8, 2, 16, 128), vm(8, 2, 16, 128),
            pltpu.SemaphoreType.DMA((10,)), pltpu.SemaphoreType.DMA((sems,)), pltpu.SemaphoreType.DMA((sems,)),
        ],
        compiler_params=pltpu.CompilerParams(
            collective_id=0, has_side_effects=True, vmem_limit_bytes=48 * 1024 * 1024
        ),
        name="exchange",
    )(pressure, *tabs)
    return tuple(
        pl.pallas_call(
            write_kernel,
            out_shape=[jax.ShapeDtypeStruct(s, F32) for s in OUTS],
            in_specs=[VM] * 4,
            out_specs=[ANY] * 4,
            scratch_shapes=[pltpu.VMEM(OUTS[3], F32), pltpu.SemaphoreType.DMA((4,))],
            compiler_params=pltpu.CompilerParams(vmem_limit_bytes=16 * 1024 * 1024),
            name="write",
        )(*mid)
    )


def solution(mesh):
    return jax.shard_map(
        per_device,
        mesh=mesh,
        in_specs=(P("wide", "narrow", None),),
        out_specs=(
            P(None, "wide", "narrow", None),
            P(None, "wide", "narrow", None),
            P(None, "wide", "narrow", None),
            P(None, None, "narrow", None),
        ),
        check_vma=False,
    )
```

```python
import jax
import jax.numpy as jnp
import ml_dtypes
import numpy as np
from jax import lax
from jax.experimental import pallas as pl
from jax.experimental.pallas import tpu as pltpu
from jax.sharding import PartitionSpec as P

MESH = pl.DeviceIdType.MESH
F32, BF16 = jnp.float32, jnp.bfloat16

LA = -1.586134342
LB = -0.05298011854
LG = 0.8829110762
LD = 0.4435068522
LZ = 1.149604398
LI = 1.0 / 1.149604398


def lift_matrix(n):
    v = np.eye(n)
    s, d = v[0::2].copy(), v[1::2].copy()

    def nxt(q):
        return np.concatenate([q[1:], q[-1:]])

    def prv(q):
        return np.concatenate([q[:1], q[:-1]])

    d = d + LA * (s + nxt(s))
    s = s + LB * (prv(d) + d)
    d = d + LG * (s + nxt(s))
    s = s + LD * (prv(d) + d)
    return np.concatenate([s * LZ, d * LI])


def chain():
    out, low = {}, np.eye(512)
    for k in (1, 2, 3, 4):
        out[k] = lift_matrix(1024 >> k) @ low
        low = out[k][: 512 >> k]
    return out


CH = chain()
L64 = lift_matrix(64)
H_LOW = [float(L64[16, 32 + k]) for k in range(5)]
H_HIGH = [float(L64[48, 33 + k]) for k in range(4)]


def two(a):
    hi = a.astype(ml_dtypes.bfloat16)
    return hi, (a - hi.astype(np.float64)).astype(ml_dtypes.bfloat16)


def stack_rhs(a):
    hi, lo = two(a)
    return np.concatenate([hi, hi, lo], axis=0)


def stack_lhs(a):
    hi, lo = two(a)
    return np.concatenate([hi, hi, lo], axis=-1)


def y_rows(k, n):
    half, own = 512 >> k, 64 >> k
    return list(range(n * own, (n + 1) * own)) + list(range(half + n * own, half + (n + 1) * own))


def y_block(k, to, cells, rows):
    if not 0 <= to < 8:
        return np.zeros((len(rows), 64))
    return CH[k][[y_rows(k, to)[r] for r in rows]][:, 64 * cells : 64 * cells + 64]


def y_table(k, n):
    own = 64 >> k
    up = list(range(4)) + list(range(own, own + 4))
    down = list(range(2 * own - 4, 2 * own)) + list(range(own - 4, own))
    for to, rows in ((n + 1, up), (n - 1, down)):
        if 0 <= to < 8:
            rest = [r for r in range(2 * own) if r not in rows]
            assert not rest or abs(y_block(k, to, n, rest)).max() < 1e-15
    return np.concatenate(
        [y_block(k, n, n, list(range(2 * own))), y_block(k, n + 1, n, up), y_block(k, n - 1, n, down)]
    )


def y4_table(n):
    rows = np.concatenate([y_block(4, to, n, list(range(8))) for to in (n, n + 1, n - 1)])
    return np.einsum("ry,pq->rpqy", rows, np.eye(8)).reshape(24 * 8, 512)


def tables():
    x4 = CH[4].T
    t = {}
    t["x34"] = stack_rhs(np.concatenate([CH[3].T, x4, x4], axis=1))
    t["x2"] = stack_rhs(CH[2].T)
    t["x1"] = stack_rhs(CH[1].T)
    t["y4"] = np.stack([stack_lhs(y4_table(n)) for n in (0, 3, 7)])
    t["y3"] = np.stack([stack_lhs(y_table(3, n)) for n in range(8)])
    t["y2"] = np.stack([stack_lhs(y_table(2, n)) for n in range(8)])
    low3 = CH[3][:64]
    ca = np.zeros((8, 16, 64))
    fin = np.zeros((64, 128))
    for y in range(8):
        for s in range(15):
            w = 8 * y - 3 + s
            if 0 <= w < 64:
                ca[y, s] = low3[w, 64 * y : 64 * y + 64]
                fin[:, 16 * y + s] = L64[:, w]
        for w in range(64):
            if not 8 * y - 3 <= w <= 8 * y + 11:
                assert abs(low3[w, 64 * y : 64 * y + 64]).max() < 1e-15
    t["ca"] = np.stack([stack_lhs(ca[y]) for y in range(8)])
    t["fin"] = stack_lhs(fin)
    c3 = np.zeros((64, 8, 2, 8))
    for w in range(64):
        for i in range(8):
            to = w + i - 3
            if 0 <= to < 64:
                c3[w, i, 0] = CH[3][to, 8 * w : 8 * w + 8]
                c3[w, i, 1] = CH[3][64 + to, 8 * w : 8 * w + 8]
    for w in range(4, 60):
        assert abs(c3[w] - c3[30]).max() < 1e-15
    c3 = c3[[0, 1, 2, 3, 30, 60, 61, 62, 63]].reshape(9, 128, 1)
    t["c3"] = np.concatenate([np.repeat(h, 128, axis=2) for h in two(c3)], axis=2)
    return t


def pack(t):
    blocks = {
        "x1": t["x1"],
        "xs": np.concatenate([t["x34"], t["x2"]], axis=1),
        "y4": t["y4"].reshape(3, 192, 3, 512).transpose(0, 2, 1, 3).reshape(-1, 512),
        "y2": t["y2"].reshape(-1, 192),
        "y3": t["y3"].reshape(-1, 192),
        "ca": t["ca"].reshape(-1, 192),
        "fin": t["fin"],
        "c3": t["c3"].reshape(-1, 256),
    }
    at, row, rows = {}, 0, []
    for name, block in blocks.items():
        at[name] = row
        row += block.shape[0]
        rows.append(np.pad(block, ((0, 0), (0, 512 - block.shape[1]))))
    return np.concatenate(rows, axis=0), at


TAB, AT = pack(tables())


def halves(x):
    hi = x.astype(BF16)
    return hi, (x - hi.astype(F32)).astype(BF16)


def data_rhs(x):
    hi, lo = halves(x)
    return jnp.concatenate([hi, lo, hi], axis=0)


def dot(a, b):
    return jnp.dot(a, b, preferred_element_type=F32)


def z_states(planes):
    s0, d0, s1 = planes[0], planes[1], planes[2]
    p1 = s0 + LB * (d0 + LA * (s0 + s1))
    sl, dl = planes[-2], planes[-1]
    u1 = dl + LA * sl
    u2 = sl + LB * (planes[-3] + LA * (planes[-4] + sl))
    return (s0, p1), (u1, u2)


def z_lift(planes, p0, p1, u1, u2, first, last, need_high):
    s, d = planes[0::2], planes[1::2]
    m = len(s)
    n0 = jnp.where(last, s[-1], p0)
    d = [d[i] + LA * (s[i] + (s[i + 1] if i + 1 < m else n0)) for i in range(m)]
    before = jnp.where(first, d[0], u1 + LA * s[0])
    s_old = s
    s = [s[i] + LB * ((d[i - 1] if i else before) + d[i]) for i in range(m)]
    n1 = jnp.where(last, s[-1], p1 + LB * d[-1])
    d1 = d
    d = [d[i] + LG * (s[i] + (s[i + 1] if i + 1 < m else n1)) for i in range(m)]
    before2 = jnp.where(first, d[0], before + LG * (u2 + LB * before + s[0]))
    del s_old, d1
    low = [(s[i] + LD * ((d[i - 1] if i else before2) + d[i])) * LZ for i in range(m)]
    return low, [x * LI for x in d] if need_high else None


def main_kernel(v_hbm, tab,
                d1_o, d2_o, d3_o, f_o,
                v, vc, x34, y4, x2, y3, y2, x1, ca, fin, c3b, c3,
                so4, ri4, so3, ri3, so2, ri2, t3, t2, ga, gb, st1, zh1, e1, st2, zh2, t2b, st2b, zh2b, s3, r3,
                lsem, ss, rs):
    w, n = lax.axis_index("wide"), lax.axis_index("narrow")
    y, z = w // 8, w % 8
    wfirst, wlast = w == 0, w == 63
    nfirst, nlast = n == 0, n == 7
    n_up, n_dn = (n + 1) % 8, (n + 7) % 8
    w_up, w_dn = (w + 1) % 64, (w + 63) % 64

    loads = [pltpu.make_async_copy(v_hbm, v, lsem.at[0])]

    def load(name, index, dst, lane=0):
        rows, lanes = dst.shape
        first = AT[name] + index * rows
        if not isinstance(first, int):
            first = pl.multiple_of(first, 16)
        src = tab.at[pl.ds(first, rows), pl.ds(lane, lanes)]
        c = pltpu.make_async_copy(src, dst, lsem.at[len(loads)])
        loads.append(c)
        return c

    l_v = loads[0]
    l_x34 = load("xs", 0, x34)
    l_y4 = load("y4", jnp.minimum(n, 1) + n // 7, y4)
    l_x2 = load("xs", 0, x2, 256)
    l_y3 = load("y3", n, y3)
    l_y2 = load("y2", n, y2)
    l_c3 = load("c3", jnp.minimum(w, 4) + jnp.maximum(w - 59, 0), c3b)
    l_ca = load("ca", y, ca)
    l_x1 = load("x1", 0, x1)
    l_fin = load("fin", 0, fin)
    for c in loads:
        c.start()

    barrier = pltpu.get_barrier_semaphore()
    peers = [(w, n_up), (w, n_dn)]
    peers += [((w + 64 + d) % 64, n) for d in (1, -1, 2, -2, 3, -3, 4, -4)]
    peers += [(y * 8 + (z + d) % 8, n) for d in range(1, 8)]
    peers += [(((y + d) % 8) * 8 + z, n) for d in range(1, 8)]
    for p in peers:
        pl.semaphore_signal(barrier, inc=1, device_id=p, device_id_type=MESH)

    count = [0]
    started = []

    def send(src, dst, to):
        k = count[0]
        count[0] += 1
        c = pltpu.make_async_remote_copy(
            src_ref=src, dst_ref=dst, send_sem=ss.at[k], recv_sem=rs.at[k], device_id=to, device_id_type=MESH
        )
        c.start()
        started.append(c)
        return c

    l_v.wait()
    hi, lo = halves(v[...].reshape(512, 512))
    vc[:, 0:512] = hi
    vc[:, 512:1024] = lo
    vc[:, 1024:1536] = hi
    l_x34.wait()
    xa = dot(vc[...], x34[...])
    l_y4.wait()
    hi, lo = halves(xa[:, 128:256])
    o4 = dot(y4[0:192], hi) + dot(y4[192:384], lo) + dot(y4[384:576], hi)
    o4 = o4.reshape(24, 8, 128)
    lane_low = lax.broadcasted_iota(jnp.int32, (8, 128), 1) < 64

    def packed(base):
        return [jnp.where(lane_low, o4[base + r], o4[base + 4 + r]) for r in range(4)]

    own4, up4, dn4 = packed(0), packed(8), packed(16)
    for r in range(4):
        so4[0, r] = up4[r]
        so4[1, r] = dn4[r]

    pl.semaphore_wait(barrier, len(peers))
    a4 = [send(so4.at[0], ri4.at[0], (w, n_up)), send(so4.at[1], ri4.at[1], (w, n_dn))]

    (q0, q1), (q2, q3) = z_states([v[i] for i in range(8)])
    st1[0], st1[1], st1[2], st1[3] = q0, q1, q2, q3
    a1 = [
        send(st1.at[pl.ds(0, 2)], zh1.at[pl.ds(0, 2)], (w_dn, n)),
        send(st1.at[pl.ds(2, 2)], zh1.at[pl.ds(2, 2)], (w_up, n)),
    ]

    l_y3.wait()
    for p in range(8):
        o = dot(y3[:, 0:192], data_rhs(xa[64 * p : 64 * p + 64, 0:128]))
        t3[p] = o[0:16]
        so3[0, p] = o[16:24]
        so3[1, p] = o[24:32]
    a3 = [send(so3.at[0], ri3.at[0], (w, n_up)), send(so3.at[1], ri3.at[1], (w, n_dn))]
    l_x2.wait()
    l_y2.wait()
    xb = dot(vc[...], x2[...])
    for p in range(8):
        o = dot(y2[:, 0:192], data_rhs(xb[64 * p : 64 * p + 64]))
        t2[p] = o[0:32]
        so2[0, p] = o[32:40]
        so2[1, p] = o[40:48]
    a2 = [send(so2.at[0], ri2.at[0], (w, n_up)), send(so2.at[1], ri2.at[1], (w, n_dn))]

    for c in a4:
        c.wait_recv()
    here = pl.ds(pl.multiple_of(z * 8, 8), 8)
    for r in range(4):
        add = jnp.where(nfirst, 0.0, ri4[0, r]) + jnp.where(nlast, 0.0, ri4[1, r])
        ga[r, here, :] = own4[r] + add
    ga_sends = [
        send(ga.at[:, here, :], ga.at[:, here, :], (y * 8 + (z + d) % 8, n)) for d in (4, 3, 5, 2, 6, 1, 7)
    ]

    def add_parts(t, ri, own):
        width = t.shape[-1]
        sub_low = lax.broadcasted_iota(jnp.int32, (8, width), 0) < 4
        for p in range(8):
            up = jnp.where(nfirst, 0.0, ri[0, p])
            dn = jnp.where(nlast, 0.0, ri[1, p])
            up_r, dn_r = pltpu.roll(up, 4, 0), pltpu.roll(dn, 4, 0)
            t[p, 0:8] = t[p, 0:8] + jnp.where(sub_low, up, 0.0)
            t[p, own : own + 8] = t[p, own : own + 8] + jnp.where(sub_low, up_r, 0.0)
            t[p, own - 8 : own] = t[p, own - 8 : own] + jnp.where(sub_low, 0.0, dn)
            t[p, 2 * own - 8 : 2 * own] = t[p, 2 * own - 8 : 2 * own] + jnp.where(sub_low, 0.0, dn_r)

    for c in a2:
        c.wait_recv()
    add_parts(t2, ri2, 16)
    (q0, q1), (q2, q3) = z_states([t2[i] for i in range(8)])
    st2[0], st2[1], st2[2], st2[3] = q0, q1, q2, q3
    b2 = [
        send(st2.at[pl.ds(0, 2)], zh2.at[pl.ds(0, 2)], (w_dn, n)),
        send(st2.at[pl.ds(2, 2)], zh2.at[pl.ds(2, 2)], (w_up, n)),
    ]

    l_ca.wait()
    for c in ga_sends:
        c.wait_recv()
    cat = jnp.concatenate([ga[r] for r in range(4)], axis=1)
    part = dot(ca[:, 0:192], data_rhs(cat))
    for r in range(4):
        gb[y, r] = part[:, 128 * r : 128 * r + 128]
    gb_sends = [send(gb.at[y], gb.at[y], (((y + d) % 8) * 8 + z, n)) for d in (4, 3, 5, 2, 6, 1, 7)]

    for c in a1:
        c.wait_recv()
    for q in range(8):
        rows = slice(8 * q, 8 * q + 8)
        low, high = z_lift(
            [v[i, rows] for i in range(8)], zh1[0, rows], zh1[1, rows], zh1[2, rows], zh1[3, rows], wfirst, wlast, True
        )
        for i in range(4):
            v[i, rows] = low[i]
            v[4 + i, rows] = high[i]
    hi, lo = halves(v[...].reshape(512, 512))
    vc[:, 0:512] = hi
    vc[:, 512:1024] = lo
    vc[:, 1024:1536] = hi
    l_x1.wait()
    for h in range(2):
        o = dot(vc[...], x1[:, 256 * h : 256 * h + 256]).reshape(8, 64, 256)
        for q in range(2):
            e1[2 * h + q, :, 8:72, :] = o[:, :, 128 * q : 128 * q + 128]
    c1 = [
        send(e1.at[:, :, pl.ds(64, 8), :], e1.at[:, :, pl.ds(0, 8), :], (w, n_up)),
        send(e1.at[:, :, pl.ds(8, 8), :], e1.at[:, :, pl.ds(72, 8), :], (w, n_dn)),
    ]

    for c in b2:
        c.wait_recv()
    low, _ = z_lift([t2[i] for i in range(8)], zh2[0], zh2[1], zh2[2], zh2[3], wfirst, wlast, False)
    (q0, q1), (q2, q3) = z_states(low)
    for i in range(4):
        t2b[i] = low[i]
    st2b[0], st2b[1], st2b[2], st2b[3] = q0, q1, q2, q3
    c2 = [
        send(st2b.at[pl.ds(0, 2)], zh2b.at[pl.ds(0, 2)], (w_dn, n)),
        send(st2b.at[pl.ds(2, 2)], zh2b.at[pl.ds(2, 2)], (w_up, n)),
    ]

    for c in a3:
        c.wait_recv()
    add_parts(t3, ri3, 8)
    l_c3.wait()
    c3[...] = c3b[:, 0:128].astype(F32) + c3b[:, 128:256].astype(F32)
    planes3 = [t3[p] for p in range(8)]
    b3 = []
    for i in (7, 6, 5, 4, 2, 1, 0, 3):
        for j in range(2):
            k = i * 16 + j * 8
            acc = planes3[0] * c3[k : k + 1]
            for p in range(1, 8):
                acc = acc + planes3[p] * c3[k + p : k + p + 1]
            s3[i, j] = acc
        if i != 3:
            b3.append(send(s3.at[i], r3.at[i], ((w + 64 + i - 3) % 64, n)))

    for c in c1:
        c.wait_recv()

    @pl.when(nfirst)
    def _():
        for k in range(1, 5):
            e1[:, :, 8 - k : 9 - k, :] = e1[:, :, 8 + k : 9 + k, :]

    @pl.when(nlast)
    def _():
        for k in range(1, 5):
            e1[:, :, 71 + k : 72 + k, :] = e1[:, :, 71 - k : 72 - k, :]

    def tap(c, i, off):
        return e1[c, i, pl.ds(8 + off, 32, stride=2), :]

    for i in range(8):
        bz, zz = i // 4, i % 4
        for c in range(4):
            bx, cols = c // 2, slice(128 * (c % 2), 128 * (c % 2) + 128)
            if bz or bx:
                low = H_LOW[0] * tap(c, i, 0)
                for k in range(1, 5):
                    low = low + H_LOW[k] * (tap(c, i, -k) + tap(c, i, k))
                d1_o[4 * bz + bx - 1, zz, :, cols] = low
            high = H_HIGH[0] * tap(c, i, 1)
            for k in range(1, 4):
                high = high + H_HIGH[k] * (tap(c, i, 1 - k) + tap(c, i, 1 + k))
            d1_o[4 * bz + 2 + bx - 1, zz, :, cols] = high

    for c in b3:
        c.wait_recv()
    for j in range(2):
        acc = s3[3, j]
        for i in range(8):
            if i != 3:
                src = w - (i - 3)
                acc = acc + jnp.where((src >= 0) & (src < 64), r3[i, j], 0.0)
        for b in range(4):
            band = 4 * j + b
            if band:
                rows = slice(8 * (b // 2), 8 * (b // 2) + 8)
                cols = slice(64 * (b % 2), 64 * (b % 2) + 64)
                d3_o[band - 1, 0] = acc[rows, cols]

    for c in c2:
        c.wait_recv()
    low, high = z_lift([t2b[i] for i in range(4)], zh2b[0], zh2b[1], zh2b[2], zh2b[3], wfirst, wlast, True)
    for band in range(1, 8):
        src = high if band >= 4 else low
        by, bx = (band // 2) % 2, band % 2
        for i in range(2):
            d2_o[band - 1, i] = src[i][16 * by : 16 * by + 16, 128 * bx : 128 * bx + 128]

    l_fin.wait()
    for c in gb_sends:
        c.wait_recv()
    cat = jnp.concatenate([gb[:, r].reshape(128, 128) for r in range(4)], axis=1)
    f_o[...] = dot(fin[...], data_rhs(cat))

    for c in started:
        c.wait_send()


def write_kernel(d1, d2, d3, f, o1, o2, o3, o4, buf, sem):
    copies = [pltpu.make_async_copy(a, b, sem.at[i]) for i, (a, b) in enumerate(((d1, o1), (d2, o2), (d3, o3)))]
    for c in copies:
        c.start()
    for bz in range(2):
        for r in range(4):
            tile = f[32 * bz : 32 * bz + 32, 128 * r : 128 * r + 128]
            for b in range(4):
                buf[4 * bz + b, :, r, :] = tile[:, 32 * b : 32 * b + 32]
    last = pltpu.make_async_copy(buf, o4, sem.at[3])
    last.start()
    for c in copies + [last]:
        c.wait()


VM, ANY = pl.BlockSpec(memory_space=pltpu.VMEM), pl.BlockSpec(memory_space=pl.ANY)
OUTS = ((7, 4, 32, 256), (7, 2, 16, 128), (7, 1, 8, 64), (8, 32, 4, 32))


def per_device(pressure):
    vm = lambda *s: pltpu.VMEM(s, F32)
    vb = lambda *s: pltpu.VMEM(s, BF16)
    sems = 64
    mids = OUTS[:3] + ((64, 512),)
    mid = pl.pallas_call(
        main_kernel,
        out_shape=[jax.ShapeDtypeStruct(s, F32) for s in mids],
        in_specs=[ANY] * 2,
        out_specs=[VM] * 4,
        scratch_shapes=[
            vm(8, 64, 512), vb(512, 1536),
            vb(1536, 256), vb(576, 512), vb(1536, 256), vb(32, 256), vb(48, 256), vb(1536, 512),
            vb(16, 256), vb(64, 384), vb(128, 256), vm(128, 128),
            vm(2, 4, 8, 128), vm(2, 4, 8, 128), vm(2, 8, 8, 128), vm(2, 8, 8, 128), vm(2, 8, 8, 256), vm(2, 8, 8, 256),
            vm(8, 16, 128), vm(8, 32, 256), vm(4, 64, 128), vm(8, 4, 16, 128),
            vm(4, 64, 512), vm(4, 64, 512), vm(4, 8, 80, 128),
            vm(4, 32, 256), vm(4, 32, 256), vm(4, 32, 256), vm(4, 32, 256), vm(4, 32, 256),
            vm(8, 2, 16, 128), vm(8, 2, 16, 128),
            pltpu.SemaphoreType.DMA((10,)), pltpu.SemaphoreType.DMA((sems,)), pltpu.SemaphoreType.DMA((sems,)),
        ],
        compiler_params=pltpu.CompilerParams(
            collective_id=0, has_side_effects=True, vmem_limit_bytes=52 * 1024 * 1024
        ),
        name="exchange",
    )(pressure, jnp.asarray(TAB))
    return tuple(
        pl.pallas_call(
            write_kernel,
            out_shape=[jax.ShapeDtypeStruct(s, F32) for s in OUTS],
            in_specs=[VM] * 4,
            out_specs=[ANY] * 4,
            scratch_shapes=[pltpu.VMEM(OUTS[3], F32), pltpu.SemaphoreType.DMA((4,))],
            compiler_params=pltpu.CompilerParams(vmem_limit_bytes=16 * 1024 * 1024),
            name="write",
        )(*mid)
    )


def solution(mesh):
    return jax.shard_map(
        per_device,
        mesh=mesh,
        in_specs=(P("wide", "narrow", None),),
        out_specs=(
            P(None, "wide", "narrow", None),
            P(None, "wide", "narrow", None),
            P(None, "wide", "narrow", None),
            P(None, None, "narrow", None),
        ),
        check_vma=False,
    )
```

```python
import jax
import jax.numpy as jnp
import ml_dtypes
import numpy as np
from jax import lax
from jax.experimental import pallas as pl
from jax.experimental.pallas import tpu as pltpu
from jax.sharding import PartitionSpec as P

MESH = pl.DeviceIdType.MESH
F32, BF16 = jnp.float32, jnp.bfloat16

LA = -1.586134342
LB = -0.05298011854
LG = 0.8829110762
LD = 0.4435068522
LZ = 1.149604398
LI = 1.0 / 1.149604398


def lift_matrix(n):
    v = np.eye(n)
    s, d = v[0::2].copy(), v[1::2].copy()

    def nxt(q):
        return np.concatenate([q[1:], q[-1:]])

    def prv(q):
        return np.concatenate([q[:1], q[:-1]])

    d = d + LA * (s + nxt(s))
    s = s + LB * (prv(d) + d)
    d = d + LG * (s + nxt(s))
    s = s + LD * (prv(d) + d)
    return np.concatenate([s * LZ, d * LI])


def chain():
    out, low = {}, np.eye(512)
    for k in (1, 2, 3, 4):
        out[k] = lift_matrix(1024 >> k) @ low
        low = out[k][: 512 >> k]
    return out


CH = chain()
L64 = lift_matrix(64)
H_LOW = [float(L64[16, 32 + k]) for k in range(5)]
H_HIGH = [float(L64[48, 33 + k]) for k in range(4)]


def two(a):
    hi = a.astype(ml_dtypes.bfloat16)
    return hi, (a - hi.astype(np.float64)).astype(ml_dtypes.bfloat16)


def stack_rhs(a):
    hi, lo = two(a)
    return np.concatenate([hi, hi, lo], axis=0)


def stack_lhs(a):
    hi, lo = two(a)
    return np.concatenate([hi, hi, lo], axis=-1)


def y_rows(k, n):
    half, own = 512 >> k, 64 >> k
    return list(range(n * own, (n + 1) * own)) + list(range(half + n * own, half + (n + 1) * own))


def y_block(k, to, cells, rows):
    if not 0 <= to < 8:
        return np.zeros((len(rows), 64))
    return CH[k][[y_rows(k, to)[r] for r in rows]][:, 64 * cells : 64 * cells + 64]


def y_table(k, n):
    own = 64 >> k
    up = list(range(4)) + list(range(own, own + 4))
    down = list(range(2 * own - 4, 2 * own)) + list(range(own - 4, own))
    for to, rows in ((n + 1, up), (n - 1, down)):
        if 0 <= to < 8:
            rest = [r for r in range(2 * own) if r not in rows]
            assert not rest or abs(y_block(k, to, n, rest)).max() < 1e-15
    return np.concatenate(
        [y_block(k, n, n, list(range(2 * own))), y_block(k, n + 1, n, up), y_block(k, n - 1, n, down)]
    )


def y4_table(n):
    rows = np.concatenate([y_block(4, to, n, list(range(8))) for to in (n, n + 1, n - 1)])
    return np.einsum("ry,pq->rpqy", rows, np.eye(8)).reshape(24 * 8, 512)


def tables():
    x4 = CH[4].T
    t = {}
    t["x4"] = stack_rhs(np.concatenate([x4, x4], axis=1))
    second = lift_matrix(256)
    third = lift_matrix(128) @ second[:128]
    t["x23"] = stack_rhs(np.concatenate([second.T, third.T], axis=1))
    t["x1"] = stack_rhs(CH[1].T)
    t["y4"] = np.stack([stack_lhs(y4_table(n)) for n in (0, 3, 7)])
    t["y3"] = np.stack([stack_lhs(y_table(3, n)) for n in range(8)])
    t["y2"] = np.stack([stack_lhs(y_table(2, n)) for n in range(8)])
    low3 = CH[3][:64]
    ca = np.zeros((8, 16, 64))
    fin = np.zeros((64, 128))
    for y in range(8):
        for s in range(15):
            w = 8 * y - 3 + s
            if 0 <= w < 64:
                ca[y, s] = low3[w, 64 * y : 64 * y + 64]
                fin[:, 16 * y + s] = L64[:, w]
        for w in range(64):
            if not 8 * y - 3 <= w <= 8 * y + 11:
                assert abs(low3[w, 64 * y : 64 * y + 64]).max() < 1e-15
    t["ca"] = np.stack([stack_lhs(ca[y]) for y in range(8)])
    t["fin"] = stack_lhs(fin)
    c3 = np.zeros((64, 8, 2, 4))
    for w in range(64):
        for i in range(7):
            to = w + i - 3
            if 0 <= to < 64:
                c3[w, i, 0] = third[to, 4 * w : 4 * w + 4]
                c3[w, i, 1] = third[64 + to, 4 * w : 4 * w + 4]
        for to in range(64):
            if abs(to - w) > 3:
                assert abs(third[[to, 64 + to], 4 * w : 4 * w + 4]).max() < 1e-15
    for w in range(4, 60):
        assert abs(c3[w] - c3[30]).max() < 1e-15
    c3 = c3[[0, 1, 2, 3, 30, 60, 61, 62, 63]].reshape(9, 64, 1)
    t["c3"] = np.concatenate([np.repeat(h, 128, axis=2) for h in two(c3)], axis=2)
    return t


def pack(t):
    blocks = {
        "x1": t["x1"],
        "xs": np.concatenate([t["x4"], np.pad(t["x23"], ((0, 768), (0, 0)))], axis=1),
        "y4": t["y4"].reshape(3, 192, 3, 512).transpose(0, 2, 1, 3).reshape(-1, 512),
        "y2": t["y2"].reshape(-1, 192),
        "y3": t["y3"].reshape(-1, 192),
        "ca": t["ca"].reshape(-1, 192),
        "fin": t["fin"],
        "c3": t["c3"].reshape(-1, 256),
    }
    at, row, rows = {}, 0, []
    for name, block in blocks.items():
        at[name] = row
        row += block.shape[0]
        rows.append(np.pad(block, ((0, 0), (0, 512 - block.shape[1]))))
    return np.concatenate(rows, axis=0), at


TAB, AT = pack(tables())


def halves(x):
    hi = x.astype(BF16)
    return hi, (x - hi.astype(F32)).astype(BF16)


def data_rhs(x):
    hi, lo = halves(x)
    return jnp.concatenate([hi, lo, hi], axis=0)


def dot(a, b):
    return jnp.dot(a, b, preferred_element_type=F32)


def z_states(planes):
    s0, d0, s1 = planes[0], planes[1], planes[2]
    p1 = s0 + LB * (d0 + LA * (s0 + s1))
    sl, dl = planes[-2], planes[-1]
    u1 = dl + LA * sl
    u2 = sl + LB * (planes[-3] + LA * (planes[-4] + sl))
    return (s0, p1), (u1, u2)


def z_lift(planes, p0, p1, u1, u2, first, last, need_high):
    s, d = planes[0::2], planes[1::2]
    m = len(s)
    n0 = jnp.where(last, s[-1], p0)
    d = [d[i] + LA * (s[i] + (s[i + 1] if i + 1 < m else n0)) for i in range(m)]
    before = jnp.where(first, d[0], u1 + LA * s[0])
    s_old = s
    s = [s[i] + LB * ((d[i - 1] if i else before) + d[i]) for i in range(m)]
    n1 = jnp.where(last, s[-1], p1 + LB * d[-1])
    d1 = d
    d = [d[i] + LG * (s[i] + (s[i + 1] if i + 1 < m else n1)) for i in range(m)]
    before2 = jnp.where(first, d[0], before + LG * (u2 + LB * before + s[0]))
    del s_old, d1
    low = [(s[i] + LD * ((d[i - 1] if i else before2) + d[i])) * LZ for i in range(m)]
    return low, [x * LI for x in d] if need_high else None


def main_kernel(v_hbm, tab,
                d1_o, d2_o, d3_o, f_o,
                raw, v, vc, x4, y4, x23, y3, y2, x1, ca, fin, c3b, c3,
                so4, ri4, so23, ri23, t3, t2, ga, gb, st1, zh1, e1, st2, zh2, s3, r3,
                lsem, ss, rs):
    w, n = lax.axis_index("wide"), lax.axis_index("narrow")
    y, z = w // 8, w % 8
    wfirst, wlast = w == 0, w == 63
    nfirst, nlast = n == 0, n == 7
    n_up, n_dn = (n + 1) % 8, (n + 7) % 8
    w_up, w_dn = (w + 1) % 64, (w + 63) % 64

    loads = [pltpu.make_async_copy(v_hbm, raw, lsem.at[0])]

    def load(name, index, dst, lane=0):
        rows, lanes = dst.shape
        first = AT[name] + index * rows
        if not isinstance(first, int):
            first = pl.multiple_of(first, 16)
        src = tab.at[pl.ds(first, rows), pl.ds(lane, lanes)]
        c = pltpu.make_async_copy(src, dst, lsem.at[len(loads)])
        loads.append(c)
        return c

    l_v = loads[0]
    l_x4 = load("xs", 0, x4)
    l_y4 = load("y4", jnp.minimum(n, 1) + n // 7, y4)
    l_x1 = load("x1", 0, x1)
    l_x23 = load("xs", 0, x23, 128)
    l_y3 = load("y3", n, y3)
    l_y2 = load("y2", n, y2)
    l_ca = load("ca", y, ca)
    l_c3 = load("c3", jnp.minimum(w, 4) + jnp.maximum(w - 59, 0), c3b)
    l_fin = load("fin", 0, fin)
    for c in loads:
        c.start()

    barrier = pltpu.get_barrier_semaphore()
    peers = [(w, n_up), (w, n_dn)]
    peers += [((w + 64 + d) % 64, n) for d in (1, -1, 2, -2, 3, -3)]
    peers += [(y * 8 + (z + d) % 8, n) for d in range(1, 8)]
    peers += [(((y + d) % 8) * 8 + z, n) for d in range(1, 8)]
    for p in peers:
        pl.semaphore_signal(barrier, inc=1, device_id=p, device_id_type=MESH)

    count = [0]
    started = []

    def send(src, dst, to):
        k = count[0]
        count[0] += 1
        c = pltpu.make_async_remote_copy(
            src_ref=src, dst_ref=dst, send_sem=ss.at[k], recv_sem=rs.at[k], device_id=to, device_id_type=MESH
        )
        c.start()
        started.append(c)
        return c

    l_v.wait()
    hi, lo = halves(raw[...].reshape(512, 512))
    vc[:, 0:512] = hi
    vc[:, 512:1024] = lo
    vc[:, 1024:1536] = hi
    l_x4.wait()
    hi, lo = halves(dot(vc[...], x4[...]))
    l_y4.wait()
    o4 = dot(y4[0:192], hi) + dot(y4[192:384], lo) + dot(y4[384:576], hi)
    o4 = o4.reshape(24, 8, 128)
    lane_low = lax.broadcasted_iota(jnp.int32, (8, 128), 1) < 64

    def packed(base):
        return [jnp.where(lane_low, o4[base + r], o4[base + 4 + r]) for r in range(4)]

    own4, up4, dn4 = packed(0), packed(8), packed(16)
    for r in range(4):
        so4[0, r] = up4[r]
        so4[1, r] = dn4[r]

    pl.semaphore_wait(barrier, len(peers))
    a4 = [send(so4.at[0], ri4.at[0], (w, n_up)), send(so4.at[1], ri4.at[1], (w, n_dn))]

    l_x1.wait()
    a1 = []
    for h in range(2):
        v[h] = dot(vc[...], x1[:, 256 * h : 256 * h + 256]).reshape(8, 64, 256)
        (q0, q1), (q2, q3) = z_states([v[h, i] for i in range(8)])
        st1[h, 0], st1[h, 1], st1[h, 2], st1[h, 3] = q0, q1, q2, q3
        a1.append(
            [
                send(st1.at[h, pl.ds(0, 2)], zh1.at[h, pl.ds(0, 2)], (w_dn, n)),
                send(st1.at[h, pl.ds(2, 2)], zh1.at[h, pl.ds(2, 2)], (w_up, n)),
            ]
        )

    for c in a4:
        c.wait_recv()
    here = pl.ds(pl.multiple_of(z * 8, 8), 8)
    for r in range(4):
        add = jnp.where(nfirst, 0.0, ri4[0, r]) + jnp.where(nlast, 0.0, ri4[1, r])
        ga[r, here, :] = own4[r] + add
    ga_sends = [
        send(ga.at[:, here, :], ga.at[:, here, :], (y * 8 + (z + d) % 8, n)) for d in (4, 3, 5, 2, 6, 1, 7)
    ]

    def z_of_half(h):
        for c in a1[h]:
            c.wait_recv()
        for q in range(8):
            rows = slice(8 * q, 8 * q + 8)
            low, high = z_lift(
                [v[h, i, rows] for i in range(8)],
                zh1[h, 0, rows], zh1[h, 1, rows], zh1[h, 2, rows], zh1[h, 3, rows], wfirst, wlast, True,
            )
            both = low + high
            for i in range(8):
                v[h, i, rows] = both[i]

    def y_halo(h):
        for q in range(2):
            e1[2 * h + q, :, 8:72, :] = v[h, :, :, 128 * q : 128 * q + 128]
        part = e1.at[pl.ds(2 * h, 2)]
        return [
            send(part.at[:, :, pl.ds(64, 8), :], part.at[:, :, pl.ds(0, 8), :], (w, n_up)),
            send(part.at[:, :, pl.ds(8, 8), :], part.at[:, :, pl.ds(72, 8), :], (w, n_dn)),
        ]

    z_of_half(0)
    l_x23.wait()
    hi, lo = halves(v[0, 0:4].reshape(256, 256))
    xb = dot(jnp.concatenate([hi, lo, hi], axis=1), x23[...])
    l_y2.wait()
    l_y3.wait()
    for p in range(4):
        o = dot(y2[:, 0:192], data_rhs(xb[64 * p : 64 * p + 64, 0:256]))
        t2[p] = o[0:32]
        so23[0, p, :, 0:256] = o[32:40]
        so23[1, p, :, 0:256] = o[40:48]
        o = dot(y3[:, 0:192], data_rhs(xb[64 * p : 64 * p + 64, 256:384]))
        t3[p] = o[0:16]
        so23[0, p, :, 256:384] = o[16:24]
        so23[1, p, :, 256:384] = o[24:32]
    a23 = [send(so23.at[0], ri23.at[0], (w, n_up)), send(so23.at[1], ri23.at[1], (w, n_dn))]
    c1 = [y_halo(0)]

    l_ca.wait()
    for c in ga_sends:
        c.wait_recv()
    cat = jnp.concatenate([ga[r] for r in range(4)], axis=1)
    part = dot(ca[:, 0:192], data_rhs(cat))
    for r in range(4):
        gb[y, r] = part[:, 128 * r : 128 * r + 128]
    gb_sends = [send(gb.at[y], gb.at[y], (((y + d) % 8) * 8 + z, n)) for d in (4, 3, 5, 2, 6, 1, 7)]

    def add_parts(t, cols, own):
        sub_low = lax.broadcasted_iota(jnp.int32, (8, t.shape[-1]), 0) < 4
        for p in range(4):
            up = jnp.where(nfirst, 0.0, ri23[0, p, :, cols])
            dn = jnp.where(nlast, 0.0, ri23[1, p, :, cols])
            up_r, dn_r = pltpu.roll(up, 4, 0), pltpu.roll(dn, 4, 0)
            t[p, 0:8] = t[p, 0:8] + jnp.where(sub_low, up, 0.0)
            t[p, own : own + 8] = t[p, own : own + 8] + jnp.where(sub_low, up_r, 0.0)
            t[p, own - 8 : own] = t[p, own - 8 : own] + jnp.where(sub_low, 0.0, dn)
            t[p, 2 * own - 8 : 2 * own] = t[p, 2 * own - 8 : 2 * own] + jnp.where(sub_low, 0.0, dn_r)

    for c in a23:
        c.wait_recv()
    add_parts(t2, slice(0, 256), 16)
    add_parts(t3, slice(256, 384), 8)
    (q0, q1), (q2, q3) = z_states([t2[i] for i in range(4)])
    st2[0], st2[1], st2[2], st2[3] = q0, q1, q2, q3
    b2 = [
        send(st2.at[pl.ds(0, 2)], zh2.at[pl.ds(0, 2)], (w_dn, n)),
        send(st2.at[pl.ds(2, 2)], zh2.at[pl.ds(2, 2)], (w_up, n)),
    ]
    l_c3.wait()
    c3[...] = c3b[:, 0:128].astype(F32) + c3b[:, 128:256].astype(F32)
    planes3 = [t3[p] for p in range(4)]
    b3 = []
    for i in (6, 0, 5, 1, 4, 2, 3):
        for j in range(2):
            k = i * 8 + j * 4
            acc = planes3[0] * c3[k : k + 1]
            for p in range(1, 4):
                acc = acc + planes3[p] * c3[k + p : k + p + 1]
            s3[i, j] = acc
        if i != 3:
            b3.append(send(s3.at[i], r3.at[i], ((w + 64 + i - 3) % 64, n)))

    z_of_half(1)
    c1.append(y_halo(1))

    def tap(c, i, off):
        return e1[c, i, pl.ds(8 + off, 32, stride=2), :]

    def bands_one(h):
        for c in c1[h]:
            c.wait_recv()
        own = slice(2 * h, 2 * h + 2)

        @pl.when(nfirst)
        def _():
            for k in range(1, 5):
                e1[own, :, 8 - k : 9 - k, :] = e1[own, :, 8 + k : 9 + k, :]

        @pl.when(nlast)
        def _():
            for k in range(1, 5):
                e1[own, :, 71 + k : 72 + k, :] = e1[own, :, 71 - k : 72 - k, :]

        for i in range(8):
            bz, zz = i // 4, i % 4
            for q in range(2):
                c, cols = 2 * h + q, slice(128 * q, 128 * q + 128)
                if bz or h:
                    low = H_LOW[0] * tap(c, i, 0)
                    for k in range(1, 5):
                        low = low + H_LOW[k] * (tap(c, i, -k) + tap(c, i, k))
                    d1_o[4 * bz + h - 1, zz, :, cols] = low
                high = H_HIGH[0] * tap(c, i, 1)
                for k in range(1, 4):
                    high = high + H_HIGH[k] * (tap(c, i, 1 - k) + tap(c, i, 1 + k))
                d1_o[4 * bz + 2 + h - 1, zz, :, cols] = high

    bands_one(0)
    bands_one(1)

    for c in b3:
        c.wait_recv()
    for j in range(2):
        acc = s3[3, j]
        for i in range(7):
            if i != 3:
                src = w - (i - 3)
                acc = acc + jnp.where((src >= 0) & (src < 64), r3[i, j], 0.0)
        for b in range(4):
            band = 4 * j + b
            if band:
                rows = slice(8 * (b // 2), 8 * (b // 2) + 8)
                cols = slice(64 * (b % 2), 64 * (b % 2) + 64)
                d3_o[band - 1, 0] = acc[rows, cols]

    for c in b2:
        c.wait_recv()
    low, high = z_lift([t2[i] for i in range(4)], zh2[0], zh2[1], zh2[2], zh2[3], wfirst, wlast, True)
    for band in range(1, 8):
        src = high if band >= 4 else low
        by, bx = (band // 2) % 2, band % 2
        for i in range(2):
            d2_o[band - 1, i] = src[i][16 * by : 16 * by + 16, 128 * bx : 128 * bx + 128]

    l_fin.wait()
    for c in gb_sends:
        c.wait_recv()
    cat = jnp.concatenate([gb[:, r].reshape(128, 128) for r in range(4)], axis=1)
    f_o[...] = dot(fin[...], data_rhs(cat))

    for c in started:
        c.wait_send()


def write_kernel(d1, d2, d3, f, o1, o2, o3, o4, buf, sem):
    copies = [pltpu.make_async_copy(a, b, sem.at[i]) for i, (a, b) in enumerate(((d1, o1), (d2, o2), (d3, o3)))]
    for c in copies:
        c.start()
    for bz in range(2):
        for r in range(4):
            tile = f[32 * bz : 32 * bz + 32, 128 * r : 128 * r + 128]
            for b in range(4):
                buf[4 * bz + b, :, r, :] = tile[:, 32 * b : 32 * b + 32]
    last = pltpu.make_async_copy(buf, o4, sem.at[3])
    last.start()
    for c in copies + [last]:
        c.wait()


VM, ANY = pl.BlockSpec(memory_space=pltpu.VMEM), pl.BlockSpec(memory_space=pl.ANY)
OUTS = ((7, 4, 32, 256), (7, 2, 16, 128), (7, 1, 8, 64), (8, 32, 4, 32))


def per_device(pressure):
    vm = lambda *s: pltpu.VMEM(s, F32)
    vb = lambda *s: pltpu.VMEM(s, BF16)
    sems = 64
    mids = OUTS[:3] + ((64, 512),)
    mid = pl.pallas_call(
        main_kernel,
        out_shape=[jax.ShapeDtypeStruct(s, F32) for s in mids],
        in_specs=[ANY] * 2,
        out_specs=[VM] * 4,
        scratch_shapes=[
            vm(8, 64, 512), vm(2, 8, 64, 256), vb(512, 1536),
            vb(1536, 128), vb(576, 512), vb(768, 384), vb(32, 256), vb(48, 256), vb(1536, 512),
            vb(16, 256), vb(64, 384), vb(64, 256), vm(64, 128),
            vm(2, 4, 8, 128), vm(2, 4, 8, 128), vm(2, 4, 8, 384), vm(2, 4, 8, 384),
            vm(4, 16, 128), vm(4, 32, 256), vm(4, 64, 128), vm(8, 4, 16, 128),
            vm(2, 4, 64, 256), vm(2, 4, 64, 256), vm(4, 8, 80, 128),
            vm(4, 32, 256), vm(4, 32, 256),
            vm(7, 2, 16, 128), vm(7, 2, 16, 128),
            pltpu.SemaphoreType.DMA((10,)), pltpu.SemaphoreType.DMA((sems,)), pltpu.SemaphoreType.DMA((sems,)),
        ],
        compiler_params=pltpu.CompilerParams(
            collective_id=0, has_side_effects=True, vmem_limit_bytes=52 * 1024 * 1024
        ),
        name="exchange",
    )(pressure, jnp.asarray(TAB))
    return tuple(
        pl.pallas_call(
            write_kernel,
            out_shape=[jax.ShapeDtypeStruct(s, F32) for s in OUTS],
            in_specs=[VM] * 4,
            out_specs=[ANY] * 4,
            scratch_shapes=[pltpu.VMEM(OUTS[3], F32), pltpu.SemaphoreType.DMA((4,))],
            compiler_params=pltpu.CompilerParams(vmem_limit_bytes=16 * 1024 * 1024),
            name="write",
        )(*mid)
    )


def solution(mesh):
    return jax.shard_map(
        per_device,
        mesh=mesh,
        in_specs=(P("wide", "narrow", None),),
        out_specs=(
            P(None, "wide", "narrow", None),
            P(None, "wide", "narrow", None),
            P(None, "wide", "narrow", None),
            P(None, None, "narrow", None),
        ),
        check_vma=False,
    )
```

```python
import jax
import jax.numpy as jnp
import ml_dtypes
import numpy as np
from jax import lax
from jax.experimental import pallas as pl
from jax.experimental.pallas import tpu as pltpu
from jax.sharding import PartitionSpec as P

MESH = pl.DeviceIdType.MESH
F32, BF16 = jnp.float32, jnp.bfloat16

LA = -1.586134342
LB = -0.05298011854
LG = 0.8829110762
LD = 0.4435068522
LZ = 1.149604398
LI = 1.0 / 1.149604398


def lift_matrix(n):
    v = np.eye(n)
    s, d = v[0::2].copy(), v[1::2].copy()

    def nxt(q):
        return np.concatenate([q[1:], q[-1:]])

    def prv(q):
        return np.concatenate([q[:1], q[:-1]])

    d = d + LA * (s + nxt(s))
    s = s + LB * (prv(d) + d)
    d = d + LG * (s + nxt(s))
    s = s + LD * (prv(d) + d)
    return np.concatenate([s * LZ, d * LI])


def chain():
    out, low = {}, np.eye(512)
    for k in (1, 2, 3, 4):
        out[k] = lift_matrix(1024 >> k) @ low
        low = out[k][: 512 >> k]
    return out


CH = chain()
L64 = lift_matrix(64)
H_LOW = [float(L64[16, 32 + k]) for k in range(5)]
H_HIGH = [float(L64[48, 33 + k]) for k in range(4)]


def two(a):
    hi = a.astype(ml_dtypes.bfloat16)
    return hi, (a - hi.astype(np.float64)).astype(ml_dtypes.bfloat16)


def stack_rhs(a):
    hi, lo = two(a)
    return np.concatenate([hi, hi, lo], axis=0)


def stack_lhs(a):
    hi, lo = two(a)
    return np.concatenate([hi, hi, lo], axis=-1)


def y_rows(k, n):
    half, own = 512 >> k, 64 >> k
    return list(range(n * own, (n + 1) * own)) + list(range(half + n * own, half + (n + 1) * own))


def y_block(k, to, cells, rows):
    if not 0 <= to < 8:
        return np.zeros((len(rows), 64))
    return CH[k][[y_rows(k, to)[r] for r in rows]][:, 64 * cells : 64 * cells + 64]


def y_table(k, n):
    own = 64 >> k
    up = list(range(4)) + list(range(own, own + 4))
    down = list(range(2 * own - 4, 2 * own)) + list(range(own - 4, own))
    for to, rows in ((n + 1, up), (n - 1, down)):
        if 0 <= to < 8:
            rest = [r for r in range(2 * own) if r not in rows]
            assert not rest or abs(y_block(k, to, n, rest)).max() < 1e-15
    return np.concatenate(
        [y_block(k, n, n, list(range(2 * own))), y_block(k, n + 1, n, up), y_block(k, n - 1, n, down)]
    )


def y4_table(n):
    rows = np.concatenate([y_block(4, to, n, list(range(8))) for to in (n, n + 1, n - 1)])
    return np.einsum("ry,pq->rpqy", rows, np.eye(8)).reshape(24 * 8, 512)


def tables():
    x4 = CH[4].T
    t = {}
    t["x4"] = stack_rhs(np.concatenate([x4, x4], axis=1))
    second = lift_matrix(256)
    third = lift_matrix(128) @ second[:128]
    t["x23"] = stack_rhs(np.concatenate([second.T, third.T], axis=1))
    t["x1"] = stack_rhs(CH[1].T)
    t["y4"] = np.stack([stack_lhs(y4_table(n)) for n in (0, 3, 7)])
    t["y3"] = np.stack([stack_lhs(y_table(3, n)) for n in range(8)])
    t["y2"] = np.stack([stack_lhs(y_table(2, n)) for n in range(8)])
    low3 = CH[3][:64]
    ca = np.zeros((8, 16, 64))
    fin = np.zeros((64, 128))
    for y in range(8):
        for s in range(15):
            w = 8 * y - 3 + s
            if 0 <= w < 64:
                ca[y, s] = low3[w, 64 * y : 64 * y + 64]
                fin[:, 16 * y + s] = L64[:, w]
        for w in range(64):
            if not 8 * y - 3 <= w <= 8 * y + 11:
                assert abs(low3[w, 64 * y : 64 * y + 64]).max() < 1e-15
    t["ca"] = np.stack([stack_lhs(ca[y]) for y in range(8)])
    t["fin"] = stack_lhs(fin)
    c3 = np.zeros((64, 8, 2, 4))
    for w in range(64):
        for i in range(7):
            to = w + i - 3
            if 0 <= to < 64:
                c3[w, i, 0] = third[to, 4 * w : 4 * w + 4]
                c3[w, i, 1] = third[64 + to, 4 * w : 4 * w + 4]
        assert abs(c3[w, 6, 1]).max() < 1e-15
        for to in range(64):
            if abs(to - w) > 3:
                assert abs(third[[to, 64 + to], 4 * w : 4 * w + 4]).max() < 1e-15
    for w in range(4, 60):
        assert abs(c3[w] - c3[30]).max() < 1e-15
    c3 = c3[[0, 1, 2, 3, 30, 60, 61, 62, 63]].reshape(9, 64, 1)
    t["c3"] = np.concatenate([np.repeat(h, 128, axis=2) for h in two(c3)], axis=2)
    return t


def pack(t):
    blocks = {
        "x1": t["x1"],
        "xs": np.concatenate([t["x4"], np.pad(t["x23"], ((0, 768), (0, 0)))], axis=1),
        "y4": t["y4"].reshape(3, 192, 3, 512).transpose(0, 2, 1, 3).reshape(-1, 512),
        "y2": t["y2"].reshape(-1, 192),
        "y3": t["y3"].reshape(-1, 192),
        "ca": t["ca"].reshape(-1, 192),
        "fin": t["fin"],
        "c3": t["c3"].reshape(-1, 256),
    }
    at, row, rows = {}, 0, []
    for name, block in blocks.items():
        at[name] = row
        row += block.shape[0]
        rows.append(np.pad(block, ((0, 0), (0, 512 - block.shape[1]))))
    return np.concatenate(rows, axis=0), at


TAB, AT = pack(tables())


def halves(x):
    hi = x.astype(BF16)
    return hi, (x - hi.astype(F32)).astype(BF16)


def data_rhs(x):
    hi, lo = halves(x)
    return jnp.concatenate([hi, lo, hi], axis=0)


def dot(a, b):
    return jnp.dot(a, b, preferred_element_type=F32)


def z_states(planes):
    s0, d0, s1 = planes[0], planes[1], planes[2]
    p1 = s0 + LB * (d0 + LA * (s0 + s1))
    sl, dl = planes[-2], planes[-1]
    u1 = dl + LA * sl
    u2 = sl + LB * (planes[-3] + LA * (planes[-4] + sl))
    return (s0, p1), (u1, u2)


def z_lift(planes, p0, p1, u1, u2, first, last, need_high):
    s, d = planes[0::2], planes[1::2]
    m = len(s)
    n0 = jnp.where(last, s[-1], p0)
    d = [d[i] + LA * (s[i] + (s[i + 1] if i + 1 < m else n0)) for i in range(m)]
    before = jnp.where(first, d[0], u1 + LA * s[0])
    s_old = s
    s = [s[i] + LB * ((d[i - 1] if i else before) + d[i]) for i in range(m)]
    n1 = jnp.where(last, s[-1], p1 + LB * d[-1])
    d1 = d
    d = [d[i] + LG * (s[i] + (s[i + 1] if i + 1 < m else n1)) for i in range(m)]
    before2 = jnp.where(first, d[0], before + LG * (u2 + LB * before + s[0]))
    del s_old, d1
    low = [(s[i] + LD * ((d[i - 1] if i else before2) + d[i])) * LZ for i in range(m)]
    return low, [x * LI for x in d] if need_high else None


def main_kernel(v_hbm, tab,
                d1_o, d2_o, d3_o, f_o,
                raw, v, vc, x4, y4, x23, y3, y2, x1, ca, fin, c3b, c3,
                so4, ri4, so23, ri23, t3, t2, ga, gb, st1, zh1, e1, st2, zh2, s3, r3,
                lsem, ss, rs):
    w, n = lax.axis_index("wide"), lax.axis_index("narrow")
    y, z = w // 8, w % 8
    wfirst, wlast = w == 0, w == 63
    nfirst, nlast = n == 0, n == 7
    n_up, n_dn = (n + 1) % 8, (n + 7) % 8
    w_up, w_dn = (w + 1) % 64, (w + 63) % 64

    loads = [pltpu.make_async_copy(v_hbm, raw, lsem.at[0])]

    def load(name, index, dst, lane=0):
        rows, lanes = dst.shape
        first = AT[name] + index * rows
        if not isinstance(first, int):
            first = pl.multiple_of(first, 16)
        src = tab.at[pl.ds(first, rows), pl.ds(lane, lanes)]
        c = pltpu.make_async_copy(src, dst, lsem.at[len(loads)])
        loads.append(c)
        return c

    l_v = loads[0]
    l_x4 = load("xs", 0, x4)
    l_y4 = load("y4", jnp.minimum(n, 1) + n // 7, y4)
    l_x1 = load("x1", 0, x1)
    l_x23 = load("xs", 0, x23, 128)
    l_y3 = load("y3", n, y3)
    l_y2 = load("y2", n, y2)
    l_ca = load("ca", y, ca)
    l_c3 = load("c3", jnp.minimum(w, 4) + jnp.maximum(w - 59, 0), c3b)
    l_fin = load("fin", 0, fin)
    for c in loads:
        c.start()

    barrier = pltpu.get_barrier_semaphore()
    peers = [(w, n_up), (w, n_dn)]
    peers += [((w + 64 + d) % 64, n) for d in (1, -1, 2, -2, 3, -3)]
    peers += [(y * 8 + (z + d) % 8, n) for d in range(1, 8)]
    peers += [(((y + d) % 8) * 8 + z, n) for d in range(1, 8)]
    for p in peers:
        pl.semaphore_signal(barrier, inc=1, device_id=p, device_id_type=MESH)

    count = [0]
    started = []

    def send(src, dst, to):
        k = count[0]
        count[0] += 1
        c = pltpu.make_async_remote_copy(
            src_ref=src, dst_ref=dst, send_sem=ss.at[k], recv_sem=rs.at[k], device_id=to, device_id_type=MESH
        )
        c.start()
        started.append(c)
        return c

    l_v.wait()
    hi, lo = halves(raw[...].reshape(512, 512))
    vc[:, 0:512] = hi
    vc[:, 512:1024] = lo
    vc[:, 1024:1536] = hi
    l_x4.wait()
    hi, lo = halves(dot(vc[...], x4[...]))
    l_y4.wait()
    o4 = dot(y4[0:192], hi) + dot(y4[192:384], lo) + dot(y4[384:576], hi)
    o4 = o4.reshape(24, 8, 128)
    lane_low = lax.broadcasted_iota(jnp.int32, (8, 128), 1) < 64

    def packed(base):
        return [jnp.where(lane_low, o4[base + r], o4[base + 4 + r]) for r in range(4)]

    own4, up4, dn4 = packed(0), packed(8), packed(16)
    for r in range(4):
        so4[0, r] = up4[r]
        so4[1, r] = dn4[r]

    pl.semaphore_wait(barrier, len(peers))
    a4 = [send(so4.at[0], ri4.at[0], (w, n_up)), send(so4.at[1], ri4.at[1], (w, n_dn))]

    def z_send(h):
        v[h] = dot(vc[...], x1[:, 256 * h : 256 * h + 256]).reshape(8, 64, 256)
        (q0, q1), (q2, q3) = z_states([v[h, i] for i in range(8)])
        st1[h, 0], st1[h, 1], st1[h, 2], st1[h, 3] = q0, q1, q2, q3
        return [
            send(st1.at[h, pl.ds(0, 2)], zh1.at[h, pl.ds(0, 2)], (w_dn, n)),
            send(st1.at[h, pl.ds(2, 2)], zh1.at[h, pl.ds(2, 2)], (w_up, n)),
        ]

    l_x1.wait()
    a1 = [z_send(0)]

    for c in a4:
        c.wait_recv()
    here = pl.ds(pl.multiple_of(z * 8, 8), 8)
    for r in range(4):
        add = jnp.where(nfirst, 0.0, ri4[0, r]) + jnp.where(nlast, 0.0, ri4[1, r])
        ga[r, here, :] = own4[r] + add
    ga_sends = [
        send(ga.at[:, here, :], ga.at[:, here, :], (y * 8 + (z + d) % 8, n)) for d in (1, 7, 2, 6, 3, 5, 4)
    ]

    def z_of_half(h):
        for c in a1[h]:
            c.wait_recv()
        for q in range(8):
            rows = slice(8 * q, 8 * q + 8)
            low, high = z_lift(
                [v[h, i, rows] for i in range(8)],
                zh1[h, 0, rows], zh1[h, 1, rows], zh1[h, 2, rows], zh1[h, 3, rows], wfirst, wlast, True,
            )
            both = low + high
            for i in range(8):
                v[h, i, rows] = both[i]

    def y_halo(h):
        for q in range(2):
            e1[2 * h + q, :, 8:72, :] = v[h, :, :, 128 * q : 128 * q + 128]
        part = e1.at[pl.ds(2 * h, 2)]
        return [
            send(part.at[:, :, pl.ds(64, 8), :], part.at[:, :, pl.ds(0, 8), :], (w, n_up)),
            send(part.at[:, :, pl.ds(8, 8), :], part.at[:, :, pl.ds(72, 8), :], (w, n_dn)),
        ]

    z_of_half(0)
    l_x23.wait()
    hi, lo = halves(v[0, 0:4].reshape(256, 256))
    xb = dot(jnp.concatenate([hi, lo, hi], axis=1), x23[...])
    l_y2.wait()
    l_y3.wait()
    for p in range(4):
        o = dot(y2[:, 0:192], data_rhs(xb[64 * p : 64 * p + 64, 0:256]))
        t2[p] = o[0:32]
        so23[0, p, :, 0:256] = o[32:40]
        so23[1, p, :, 0:256] = o[40:48]
        o = dot(y3[:, 0:192], data_rhs(xb[64 * p : 64 * p + 64, 256:384]))
        t3[p] = o[0:16]
        so23[0, p, :, 256:384] = o[16:24]
        so23[1, p, :, 256:384] = o[24:32]
    a23 = [send(so23.at[0], ri23.at[0], (w, n_up)), send(so23.at[1], ri23.at[1], (w, n_dn))]
    c1 = [y_halo(0)]

    a1.append(z_send(1))

    l_ca.wait()
    for c in ga_sends:
        c.wait_recv()
    cat = jnp.concatenate([ga[r] for r in range(4)], axis=1)
    part = dot(ca[:, 0:192], data_rhs(cat))
    for r in range(4):
        gb[y, r] = part[:, 128 * r : 128 * r + 128]
    gb_sends = [send(gb.at[y], gb.at[y], (((y + d) % 8) * 8 + z, n)) for d in (1, 7, 2, 6, 3, 5, 4)]

    def add_parts(t, cols, own):
        sub_low = lax.broadcasted_iota(jnp.int32, (8, t.shape[-1]), 0) < 4
        for p in range(4):
            up = jnp.where(nfirst, 0.0, ri23[0, p, :, cols])
            dn = jnp.where(nlast, 0.0, ri23[1, p, :, cols])
            up_r, dn_r = pltpu.roll(up, 4, 0), pltpu.roll(dn, 4, 0)
            t[p, 0:8] = t[p, 0:8] + jnp.where(sub_low, up, 0.0)
            t[p, own : own + 8] = t[p, own : own + 8] + jnp.where(sub_low, up_r, 0.0)
            t[p, own - 8 : own] = t[p, own - 8 : own] + jnp.where(sub_low, 0.0, dn)
            t[p, 2 * own - 8 : 2 * own] = t[p, 2 * own - 8 : 2 * own] + jnp.where(sub_low, 0.0, dn_r)

    for c in a23:
        c.wait_recv()
    add_parts(t2, slice(0, 256), 16)
    add_parts(t3, slice(256, 384), 8)
    (q0, q1), (q2, q3) = z_states([t2[i] for i in range(4)])
    st2[0], st2[1], st2[2], st2[3] = q0, q1, q2, q3
    b2 = [
        send(st2.at[pl.ds(0, 2)], zh2.at[pl.ds(0, 2)], (w_dn, n)),
        send(st2.at[pl.ds(2, 2)], zh2.at[pl.ds(2, 2)], (w_up, n)),
    ]
    l_c3.wait()
    c3[...] = c3b[:, 0:128].astype(F32) + c3b[:, 128:256].astype(F32)
    planes3 = [t3[p] for p in range(4)]
    b3 = []
    for i in (6, 0, 5, 1, 4, 2, 3):
        for j in range(2):
            k = i * 8 + j * 4
            acc = planes3[0] * c3[k : k + 1]
            for p in range(1, 4):
                acc = acc + planes3[p] * c3[k + p : k + p + 1]
            s3[i, j] = acc
        if i != 3:
            kept = pl.ds(0, 1 if i == 6 else 2)
            b3.append(send(s3.at[i, kept], r3.at[i, kept], ((w + 64 + i - 3) % 64, n)))

    z_of_half(1)
    c1.append(y_halo(1))

    def tap(c, i, off):
        return e1[c, i, pl.ds(8 + off, 32, stride=2), :]

    def bands_one(h):
        for c in c1[h]:
            c.wait_recv()
        own = slice(2 * h, 2 * h + 2)

        @pl.when(nfirst)
        def _():
            for k in range(1, 5):
                e1[own, :, 8 - k : 9 - k, :] = e1[own, :, 8 + k : 9 + k, :]

        @pl.when(nlast)
        def _():
            for k in range(1, 5):
                e1[own, :, 71 + k : 72 + k, :] = e1[own, :, 71 - k : 72 - k, :]

        for i in range(8):
            bz, zz = i // 4, i % 4
            for q in range(2):
                c, cols = 2 * h + q, slice(128 * q, 128 * q + 128)
                if bz or h:
                    low = H_LOW[0] * tap(c, i, 0)
                    for k in range(1, 5):
                        low = low + H_LOW[k] * (tap(c, i, -k) + tap(c, i, k))
                    d1_o[4 * bz + h - 1, zz, :, cols] = low
                high = H_HIGH[0] * tap(c, i, 1)
                for k in range(1, 4):
                    high = high + H_HIGH[k] * (tap(c, i, 1 - k) + tap(c, i, 1 + k))
                d1_o[4 * bz + 2 + h - 1, zz, :, cols] = high

    bands_one(0)
    bands_one(1)

    for c in b3:
        c.wait_recv()
    for j in range(2):
        acc = s3[3, j]
        for i in range(7):
            if i != 3 and not (j and i == 6):
                src = w - (i - 3)
                acc = acc + jnp.where((src >= 0) & (src < 64), r3[i, j], 0.0)
        for b in range(4):
            band = 4 * j + b
            if band:
                rows = slice(8 * (b // 2), 8 * (b // 2) + 8)
                cols = slice(64 * (b % 2), 64 * (b % 2) + 64)
                d3_o[band - 1, 0] = acc[rows, cols]

    for c in b2:
        c.wait_recv()
    low, high = z_lift([t2[i] for i in range(4)], zh2[0], zh2[1], zh2[2], zh2[3], wfirst, wlast, True)
    for band in range(1, 8):
        src = high if band >= 4 else low
        by, bx = (band // 2) % 2, band % 2
        for i in range(2):
            d2_o[band - 1, i] = src[i][16 * by : 16 * by + 16, 128 * bx : 128 * bx + 128]

    l_fin.wait()
    for c in gb_sends:
        c.wait_recv()
    cat = jnp.concatenate([gb[:, r].reshape(128, 128) for r in range(4)], axis=1)
    f_o[...] = dot(fin[...], data_rhs(cat))

    for c in started:
        c.wait_send()


def write_kernel(d1, d2, d3, f, o1, o2, o3, o4, buf, sem):
    copies = [pltpu.make_async_copy(a, b, sem.at[i]) for i, (a, b) in enumerate(((d1, o1), (d2, o2), (d3, o3)))]
    for c in copies:
        c.start()
    for bz in range(2):
        for r in range(4):
            tile = f[32 * bz : 32 * bz + 32, 128 * r : 128 * r + 128]
            for b in range(4):
                buf[4 * bz + b, :, r, :] = tile[:, 32 * b : 32 * b + 32]
        half = pl.ds(4 * bz, 4)
        c = pltpu.make_async_copy(buf.at[half], o4.at[half], sem.at[3 + bz])
        c.start()
        copies.append(c)
    for c in copies:
        c.wait()


VM, ANY = pl.BlockSpec(memory_space=pltpu.VMEM), pl.BlockSpec(memory_space=pl.ANY)
OUTS = ((7, 4, 32, 256), (7, 2, 16, 128), (7, 1, 8, 64), (8, 32, 4, 32))


def per_device(pressure):
    vm = lambda *s: pltpu.VMEM(s, F32)
    vb = lambda *s: pltpu.VMEM(s, BF16)
    sems = 64
    mids = OUTS[:3] + ((64, 512),)
    mid = pl.pallas_call(
        main_kernel,
        out_shape=[jax.ShapeDtypeStruct(s, F32) for s in mids],
        in_specs=[ANY] * 2,
        out_specs=[VM] * 4,
        scratch_shapes=[
            vm(8, 64, 512), vm(2, 8, 64, 256), vb(512, 1536),
            vb(1536, 128), vb(576, 512), vb(768, 384), vb(32, 256), vb(48, 256), vb(1536, 512),
            vb(16, 256), vb(64, 384), vb(64, 256), vm(64, 128),
            vm(2, 4, 8, 128), vm(2, 4, 8, 128), vm(2, 4, 8, 384), vm(2, 4, 8, 384),
            vm(4, 16, 128), vm(4, 32, 256), vm(4, 64, 128), vm(8, 4, 16, 128),
            vm(2, 4, 64, 256), vm(2, 4, 64, 256), vm(4, 8, 80, 128),
            vm(4, 32, 256), vm(4, 32, 256),
            vm(7, 2, 16, 128), vm(7, 2, 16, 128),
            pltpu.SemaphoreType.DMA((10,)), pltpu.SemaphoreType.DMA((sems,)), pltpu.SemaphoreType.DMA((sems,)),
        ],
        compiler_params=pltpu.CompilerParams(
            collective_id=0, has_side_effects=True, vmem_limit_bytes=52 * 1024 * 1024
        ),
        name="exchange",
    )(pressure, jnp.asarray(TAB))
    return tuple(
        pl.pallas_call(
            write_kernel,
            out_shape=[jax.ShapeDtypeStruct(s, F32) for s in OUTS],
            in_specs=[VM] * 4,
            out_specs=[ANY] * 4,
            scratch_shapes=[pltpu.VMEM(OUTS[3], F32), pltpu.SemaphoreType.DMA((5,))],
            compiler_params=pltpu.CompilerParams(vmem_limit_bytes=16 * 1024 * 1024),
            name="write",
        )(*mid)
    )


def solution(mesh):
    return jax.shard_map(
        per_device,
        mesh=mesh,
        in_specs=(P("wide", "narrow", None),),
        out_specs=(
            P(None, "wide", "narrow", None),
            P(None, "wide", "narrow", None),
            P(None, "wide", "narrow", None),
            P(None, None, "narrow", None),
        ),
        check_vma=False,
    )
```

```python
import jax
import jax.numpy as jnp
import ml_dtypes
import numpy as np
from jax import lax
from jax.experimental import pallas as pl
from jax.experimental.pallas import tpu as pltpu
from jax.sharding import PartitionSpec as P

MESH = pl.DeviceIdType.MESH
F32, BF16 = jnp.float32, jnp.bfloat16

LA = -1.586134342
LB = -0.05298011854
LG = 0.8829110762
LD = 0.4435068522
LZ = 1.149604398
LI = 1.0 / 1.149604398


def lift_matrix(n):
    v = np.eye(n)
    s, d = v[0::2].copy(), v[1::2].copy()

    def nxt(q):
        return np.concatenate([q[1:], q[-1:]])

    def prv(q):
        return np.concatenate([q[:1], q[:-1]])

    d = d + LA * (s + nxt(s))
    s = s + LB * (prv(d) + d)
    d = d + LG * (s + nxt(s))
    s = s + LD * (prv(d) + d)
    return np.concatenate([s * LZ, d * LI])


def chain():
    out, low = {}, np.eye(512)
    for k in (1, 2, 3, 4):
        out[k] = lift_matrix(1024 >> k) @ low
        low = out[k][: 512 >> k]
    return out


CH = chain()
L64 = lift_matrix(64)
H_LOW = [float(L64[16, 32 + k]) for k in range(5)]
H_HIGH = [float(L64[48, 33 + k]) for k in range(4)]


def two(a):
    hi = a.astype(ml_dtypes.bfloat16)
    return hi, (a - hi.astype(np.float64)).astype(ml_dtypes.bfloat16)


def stack_rhs(a):
    hi, lo = two(a)
    return np.concatenate([hi, hi, lo], axis=0)


def stack_lhs(a):
    hi, lo = two(a)
    return np.concatenate([hi, hi, lo], axis=-1)


def y_rows(k, n):
    half, own = 512 >> k, 64 >> k
    return list(range(n * own, (n + 1) * own)) + list(range(half + n * own, half + (n + 1) * own))


def y_block(k, to, cells, rows):
    if not 0 <= to < 8:
        return np.zeros((len(rows), 64))
    return CH[k][[y_rows(k, to)[r] for r in rows]][:, 64 * cells : 64 * cells + 64]


def y_table(k, n):
    own = 64 >> k
    up = list(range(4)) + list(range(own, own + 4))
    down = list(range(2 * own - 4, 2 * own)) + list(range(own - 4, own))
    for to, rows in ((n + 1, up), (n - 1, down)):
        if 0 <= to < 8:
            rest = [r for r in range(2 * own) if r not in rows]
            assert not rest or abs(y_block(k, to, n, rest)).max() < 1e-15
    return np.concatenate(
        [y_block(k, n, n, list(range(2 * own))), y_block(k, n + 1, n, up), y_block(k, n - 1, n, down)]
    )


def y4_table(n):
    rows = np.concatenate([y_block(4, to, n, list(range(8))) for to in (n, n + 1, n - 1)])
    return np.einsum("ry,pq->rpqy", rows, np.eye(8)).reshape(24 * 8, 512)


def tables():
    x4 = CH[4].T
    t = {}
    t["x4"] = stack_rhs(np.concatenate([x4, x4], axis=1))
    second = lift_matrix(256)
    third = lift_matrix(128) @ second[:128]
    t["x23"] = stack_rhs(np.concatenate([second.T, third.T], axis=1))
    t["x1"] = stack_rhs(CH[1].T)
    t["y4"] = np.stack([stack_lhs(y4_table(n)) for n in (0, 3, 7)])
    t["y3"] = np.stack([stack_lhs(y_table(3, n)) for n in range(8)])
    t["y2"] = np.stack([stack_lhs(y_table(2, n)) for n in range(8)])
    low3 = CH[3][:64]
    ca = np.zeros((8, 16, 64))
    fin = np.zeros((64, 128))
    for y in range(8):
        for s in range(15):
            w = 8 * y - 3 + s
            if 0 <= w < 64:
                ca[y, s] = low3[w, 64 * y : 64 * y + 64]
                fin[:, 16 * y + s] = L64[:, w]
        for w in range(64):
            if not 8 * y - 3 <= w <= 8 * y + 11:
                assert abs(low3[w, 64 * y : 64 * y + 64]).max() < 1e-15
    t["ca"] = np.stack([stack_lhs(ca[y]) for y in range(8)])
    t["fin"] = stack_lhs(fin)
    c3 = np.zeros((64, 8, 2, 4))
    for w in range(64):
        for i in range(7):
            to = w + i - 3
            if 0 <= to < 64:
                c3[w, i, 0] = third[to, 4 * w : 4 * w + 4]
                c3[w, i, 1] = third[64 + to, 4 * w : 4 * w + 4]
        assert abs(c3[w, 6, 1]).max() < 1e-15
        for to in range(64):
            if abs(to - w) > 3:
                assert abs(third[[to, 64 + to], 4 * w : 4 * w + 4]).max() < 1e-15
    for w in range(4, 60):
        assert abs(c3[w] - c3[30]).max() < 1e-15
    c3 = c3[[0, 1, 2, 3, 30, 60, 61, 62, 63]].reshape(9, 64, 1)
    t["c3"] = np.concatenate([np.repeat(h, 128, axis=2) for h in two(c3)], axis=2)
    return t


def pack(t):
    blocks = {
        "x1": t["x1"],
        "xs": np.concatenate([t["x4"], np.pad(t["x23"], ((0, 768), (0, 0)))], axis=1),
        "y4": t["y4"].reshape(3, 192, 3, 512).transpose(0, 2, 1, 3).reshape(-1, 512),
        "y2": t["y2"].reshape(-1, 192),
        "y3": t["y3"].reshape(-1, 192),
        "ca": t["ca"].reshape(-1, 192),
        "fin": t["fin"],
        "c3": t["c3"].reshape(-1, 256),
    }
    at, row, rows = {}, 0, []
    for name, block in blocks.items():
        at[name] = row
        row += block.shape[0]
        rows.append(np.pad(block, ((0, 0), (0, 512 - block.shape[1]))))
    return np.concatenate(rows, axis=0), at


TAB, AT = pack(tables())


def halves(x):
    hi = x.astype(BF16)
    return hi, (x - hi.astype(F32)).astype(BF16)


def data_rhs(x):
    hi, lo = halves(x)
    return jnp.concatenate([hi, lo, hi], axis=0)


def dot(a, b):
    return jnp.dot(a, b, preferred_element_type=F32)


def z_states(planes):
    s0, d0, s1 = planes[0], planes[1], planes[2]
    p1 = s0 + LB * (d0 + LA * (s0 + s1))
    sl, dl = planes[-2], planes[-1]
    u1 = dl + LA * sl
    u2 = sl + LB * (planes[-3] + LA * (planes[-4] + sl))
    return (s0, p1), (u1, u2)


def z_lift(planes, p0, p1, u1, u2, first, last, need_high):
    s, d = planes[0::2], planes[1::2]
    m = len(s)
    n0 = jnp.where(last, s[-1], p0)
    d = [d[i] + LA * (s[i] + (s[i + 1] if i + 1 < m else n0)) for i in range(m)]
    before = jnp.where(first, d[0], u1 + LA * s[0])
    s_old = s
    s = [s[i] + LB * ((d[i - 1] if i else before) + d[i]) for i in range(m)]
    n1 = jnp.where(last, s[-1], p1 + LB * d[-1])
    d1 = d
    d = [d[i] + LG * (s[i] + (s[i + 1] if i + 1 < m else n1)) for i in range(m)]
    before2 = jnp.where(first, d[0], before + LG * (u2 + LB * before + s[0]))
    del s_old, d1
    low = [(s[i] + LD * ((d[i - 1] if i else before2) + d[i])) * LZ for i in range(m)]
    return low, [x * LI for x in d] if need_high else None


def main_kernel(v_hbm, tab,
                d1_o, d2_o, d3_o, f_o,
                raw, v, vc, x4, y4, x23, y3, y2, x1, ca, fin, c3b, c3,
                so4, ri4, so23, ri23, t3, t2, ga, gb, st1, zh1, e1, st2, zh2, s3, r3,
                lsem, ss, rs):
    w, n = lax.axis_index("wide"), lax.axis_index("narrow")
    y, z = w // 8, w % 8
    wfirst, wlast = w == 0, w == 63
    nfirst, nlast = n == 0, n == 7
    n_up, n_dn = (n + 1) % 8, (n + 7) % 8
    w_up, w_dn = (w + 1) % 64, (w + 63) % 64

    loads = [pltpu.make_async_copy(v_hbm, raw, lsem.at[0])]

    def load(name, index, dst, lane=0):
        rows, lanes = dst.shape
        first = AT[name] + index * rows
        if not isinstance(first, int):
            first = pl.multiple_of(first, 16)
        src = tab.at[pl.ds(first, rows), pl.ds(lane, lanes)]
        c = pltpu.make_async_copy(src, dst, lsem.at[len(loads)])
        loads.append(c)
        return c

    l_v = loads[0]
    l_x4 = load("xs", 0, x4)
    l_y4 = load("y4", jnp.minimum(n, 1) + n // 7, y4)
    l_x1 = load("x1", 0, x1)
    l_x23 = load("xs", 0, x23, 128)
    l_y3 = load("y3", n, y3)
    l_y2 = load("y2", n, y2)
    l_ca = load("ca", y, ca)
    l_c3 = load("c3", jnp.minimum(w, 4) + jnp.maximum(w - 59, 0), c3b)
    l_fin = load("fin", 0, fin)
    for c in loads:
        c.start()

    barrier = pltpu.get_barrier_semaphore()
    peers = [(w, n_up), (w, n_dn)]
    peers += [((w + 64 + d) % 64, n) for d in (1, -1, 2, -2, 3, -3)]
    peers += [(y * 8 + (z + d) % 8, n) for d in range(1, 8)]
    peers += [(((y + d) % 8) * 8 + z, n) for d in range(1, 8)]
    for p in peers:
        pl.semaphore_signal(barrier, inc=1, device_id=p, device_id_type=MESH)

    count = [0]
    started = []

    def send(src, dst, to):
        k = count[0]
        count[0] += 1
        c = pltpu.make_async_remote_copy(
            src_ref=src, dst_ref=dst, send_sem=ss.at[k], recv_sem=rs.at[k], device_id=to, device_id_type=MESH
        )
        c.start()
        started.append(c)
        return c

    l_v.wait()
    hi, lo = halves(raw[...].reshape(512, 512))
    vc[:, 0:512] = hi
    vc[:, 512:1024] = lo
    vc[:, 1024:1536] = hi
    l_x4.wait()
    hi, lo = halves(dot(vc[...], x4[...]))
    l_y4.wait()
    o4 = dot(y4[0:192], hi) + dot(y4[192:384], lo) + dot(y4[384:576], hi)
    o4 = o4.reshape(24, 8, 128)
    lane_low = lax.broadcasted_iota(jnp.int32, (8, 128), 1) < 64

    def packed(base):
        return [jnp.where(lane_low, o4[base + r], o4[base + 4 + r]) for r in range(4)]

    own4, up4, dn4 = packed(0), packed(8), packed(16)
    for r in range(4):
        so4[0, r] = up4[r]
        so4[1, r] = dn4[r]

    pl.semaphore_wait(barrier, len(peers))
    a4 = [send(so4.at[0], ri4.at[0], (w, n_up)), send(so4.at[1], ri4.at[1], (w, n_dn))]

    def z_send(h):
        v[h] = dot(vc[...], x1[:, 256 * h : 256 * h + 256]).reshape(8, 64, 256)
        (q0, q1), (q2, q3) = z_states([v[h, i] for i in range(8)])
        st1[h, 0], st1[h, 1], st1[h, 2], st1[h, 3] = q0, q1, q2, q3
        return [
            send(st1.at[h, pl.ds(0, 2)], zh1.at[h, pl.ds(0, 2)], (w_dn, n)),
            send(st1.at[h, pl.ds(2, 2)], zh1.at[h, pl.ds(2, 2)], (w_up, n)),
        ]

    l_x1.wait()
    a1 = [z_send(0)]

    for c in a4:
        c.wait_recv()
    here = pl.ds(pl.multiple_of(z * 8, 8), 8)
    for r in range(4):
        add = jnp.where(nfirst, 0.0, ri4[0, r]) + jnp.where(nlast, 0.0, ri4[1, r])
        ga[r, here, :] = own4[r] + add
    ga_sends = [
        send(ga.at[:, here, :], ga.at[:, here, :], (y * 8 + (z + d) % 8, n)) for d in (1, 7, 2, 6, 3, 5, 4)
    ]

    def z_of_half(h):
        for c in a1[h]:
            c.wait_recv()
        for q in range(8):
            rows = slice(8 * q, 8 * q + 8)
            low, high = z_lift(
                [v[h, i, rows] for i in range(8)],
                zh1[h, 0, rows], zh1[h, 1, rows], zh1[h, 2, rows], zh1[h, 3, rows], wfirst, wlast, True,
            )
            both = low + high
            for i in range(8):
                v[h, i, rows] = both[i]

    def y_halo(h):
        for q in range(2):
            e1[2 * h + q, :, 8:72, :] = v[h, :, :, 128 * q : 128 * q + 128]
        part = e1.at[pl.ds(2 * h, 2)]
        return [
            send(part.at[:, :, pl.ds(64, 8), :], part.at[:, :, pl.ds(0, 8), :], (w, n_up)),
            send(part.at[:, :, pl.ds(8, 8), :], part.at[:, :, pl.ds(72, 8), :], (w, n_dn)),
        ]

    z_of_half(0)
    l_x23.wait()
    hi, lo = halves(v[0, 0:4].reshape(256, 256))
    xb = dot(jnp.concatenate([hi, lo, hi], axis=1), x23[...])
    l_y2.wait()
    l_y3.wait()
    for p in range(4):
        o = dot(y2[:, 0:192], data_rhs(xb[64 * p : 64 * p + 64, 0:256]))
        t2[p] = o[0:32]
        so23[0, p, :, 0:256] = o[32:40]
        so23[1, p, :, 0:256] = o[40:48]
        o = dot(y3[:, 0:192], data_rhs(xb[64 * p : 64 * p + 64, 256:384]))
        t3[p] = o[0:16]
        so23[0, p, :, 256:384] = o[16:24]
        so23[1, p, :, 256:384] = o[24:32]
    a23 = [send(so23.at[0], ri23.at[0], (w, n_up)), send(so23.at[1], ri23.at[1], (w, n_dn))]
    c1 = [y_halo(0)]

    a1.append(z_send(1))

    l_ca.wait()
    for c in ga_sends:
        c.wait_recv()
    cat = jnp.concatenate([ga[r] for r in range(4)], axis=1)
    part = dot(ca[:, 0:192], data_rhs(cat))
    for r in range(4):
        gb[y, r] = part[:, 128 * r : 128 * r + 128]
    gb_sends = [send(gb.at[y], gb.at[y], (((y + d) % 8) * 8 + z, n)) for d in (1, 7, 2, 6, 3, 5, 4)]

    def add_parts(t, cols, own):
        sub_low = lax.broadcasted_iota(jnp.int32, (8, t.shape[-1]), 0) < 4
        for p in range(4):
            up = jnp.where(nfirst, 0.0, ri23[0, p, :, cols])
            dn = jnp.where(nlast, 0.0, ri23[1, p, :, cols])
            up_r, dn_r = pltpu.roll(up, 4, 0), pltpu.roll(dn, 4, 0)
            t[p, 0:8] = t[p, 0:8] + jnp.where(sub_low, up, 0.0)
            t[p, own : own + 8] = t[p, own : own + 8] + jnp.where(sub_low, up_r, 0.0)
            t[p, own - 8 : own] = t[p, own - 8 : own] + jnp.where(sub_low, 0.0, dn)
            t[p, 2 * own - 8 : 2 * own] = t[p, 2 * own - 8 : 2 * own] + jnp.where(sub_low, 0.0, dn_r)

    for c in a23:
        c.wait_recv()
    add_parts(t2, slice(0, 256), 16)
    add_parts(t3, slice(256, 384), 8)
    (q0, q1), (q2, q3) = z_states([t2[i] for i in range(4)])
    st2[0], st2[1], st2[2], st2[3] = q0, q1, q2, q3
    b2 = [
        send(st2.at[pl.ds(0, 2)], zh2.at[pl.ds(0, 2)], (w_dn, n)),
        send(st2.at[pl.ds(2, 2)], zh2.at[pl.ds(2, 2)], (w_up, n)),
    ]
    l_c3.wait()
    c3[...] = c3b[:, 0:128].astype(F32) + c3b[:, 128:256].astype(F32)
    planes3 = [t3[p] for p in range(4)]
    b3 = []
    for i in (4, 2, 5, 1, 6, 0, 3):
        for j in range(2):
            k = i * 8 + j * 4
            acc = planes3[0] * c3[k : k + 1]
            for p in range(1, 4):
                acc = acc + planes3[p] * c3[k + p : k + p + 1]
            s3[i, j] = acc
        if i != 3:
            kept = pl.ds(0, 1 if i == 6 else 2)
            b3.append(send(s3.at[i, kept], r3.at[i, kept], ((w + 64 + i - 3) % 64, n)))

    z_of_half(1)
    c1.append(y_halo(1))

    def tap(c, i, off):
        return e1[c, i, pl.ds(8 + off, 32, stride=2), :]

    def bands_one(h):
        for c in c1[h]:
            c.wait_recv()
        own = slice(2 * h, 2 * h + 2)

        @pl.when(nfirst)
        def _():
            for k in range(1, 5):
                e1[own, :, 8 - k : 9 - k, :] = e1[own, :, 8 + k : 9 + k, :]

        @pl.when(nlast)
        def _():
            for k in range(1, 5):
                e1[own, :, 71 + k : 72 + k, :] = e1[own, :, 71 - k : 72 - k, :]

        for i in range(8):
            bz, zz = i // 4, i % 4
            for q in range(2):
                c, cols = 2 * h + q, slice(128 * q, 128 * q + 128)
                if bz or h:
                    low = H_LOW[0] * tap(c, i, 0)
                    for k in range(1, 5):
                        low = low + H_LOW[k] * (tap(c, i, -k) + tap(c, i, k))
                    d1_o[4 * bz + h - 1, zz, :, cols] = low
                high = H_HIGH[0] * tap(c, i, 1)
                for k in range(1, 4):
                    high = high + H_HIGH[k] * (tap(c, i, 1 - k) + tap(c, i, 1 + k))
                d1_o[4 * bz + 2 + h - 1, zz, :, cols] = high

    bands_one(0)
    bands_one(1)

    for c in b3:
        c.wait_recv()
    for j in range(2):
        acc = s3[3, j]
        for i in range(7):
            if i != 3 and not (j and i == 6):
                src = w - (i - 3)
                acc = acc + jnp.where((src >= 0) & (src < 64), r3[i, j], 0.0)
        for b in range(4):
            band = 4 * j + b
            if band:
                rows = slice(8 * (b // 2), 8 * (b // 2) + 8)
                cols = slice(64 * (b % 2), 64 * (b % 2) + 64)
                d3_o[band - 1, 0] = acc[rows, cols]

    for c in b2:
        c.wait_recv()
    low, high = z_lift([t2[i] for i in range(4)], zh2[0], zh2[1], zh2[2], zh2[3], wfirst, wlast, True)
    for band in range(1, 8):
        src = high if band >= 4 else low
        by, bx = (band // 2) % 2, band % 2
        for i in range(2):
            d2_o[band - 1, i] = src[i][16 * by : 16 * by + 16, 128 * bx : 128 * bx + 128]

    l_fin.wait()
    for c in gb_sends:
        c.wait_recv()
    cat = jnp.concatenate([gb[:, r].reshape(128, 128) for r in range(4)], axis=1)
    f_o[...] = dot(fin[...], data_rhs(cat))

    for c in started:
        c.wait_send()


def write_kernel(d1, d2, d3, f, o1, o2, o3, o4, buf, sem):
    copies = [pltpu.make_async_copy(a, b, sem.at[i]) for i, (a, b) in enumerate(((d1, o1), (d2, o2), (d3, o3)))]
    for c in copies:
        c.start()
    for bz in range(2):
        for r in range(4):
            tile = f[32 * bz : 32 * bz + 32, 128 * r : 128 * r + 128]
            for b in range(4):
                buf[4 * bz + b, :, r, :] = tile[:, 32 * b : 32 * b + 32]
        half = pl.ds(4 * bz, 4)
        c = pltpu.make_async_copy(buf.at[half], o4.at[half], sem.at[3 + bz])
        c.start()
        copies.append(c)
    for c in copies:
        c.wait()


VM, ANY = pl.BlockSpec(memory_space=pltpu.VMEM), pl.BlockSpec(memory_space=pl.ANY)
OUTS = ((7, 4, 32, 256), (7, 2, 16, 128), (7, 1, 8, 64), (8, 32, 4, 32))


def per_device(pressure):
    vm = lambda *s: pltpu.VMEM(s, F32)
    vb = lambda *s: pltpu.VMEM(s, BF16)
    sems = 64
    mids = OUTS[:3] + ((64, 512),)
    mid = pl.pallas_call(
        main_kernel,
        out_shape=[jax.ShapeDtypeStruct(s, F32) for s in mids],
        in_specs=[ANY] * 2,
        out_specs=[VM] * 4,
        scratch_shapes=[
            vm(8, 64, 512), vm(2, 8, 64, 256), vb(512, 1536),
            vb(1536, 128), vb(576, 512), vb(768, 384), vb(32, 256), vb(48, 256), vb(1536, 512),
            vb(16, 256), vb(64, 384), vb(64, 256), vm(64, 128),
            vm(2, 4, 8, 128), vm(2, 4, 8, 128), vm(2, 4, 8, 384), vm(2, 4, 8, 384),
            vm(4, 16, 128), vm(4, 32, 256), vm(4, 64, 128), vm(8, 4, 16, 128),
            vm(2, 4, 64, 256), vm(2, 4, 64, 256), vm(4, 8, 80, 128),
            vm(4, 32, 256), vm(4, 32, 256),
            vm(7, 2, 16, 128), vm(7, 2, 16, 128),
            pltpu.SemaphoreType.DMA((10,)), pltpu.SemaphoreType.DMA((sems,)), pltpu.SemaphoreType.DMA((sems,)),
        ],
        compiler_params=pltpu.CompilerParams(
            collective_id=0, has_side_effects=True, vmem_limit_bytes=52 * 1024 * 1024
        ),
        name="exchange",
    )(pressure, jnp.asarray(TAB))
    return tuple(
        pl.pallas_call(
            write_kernel,
            out_shape=[jax.ShapeDtypeStruct(s, F32) for s in OUTS],
            in_specs=[VM] * 4,
            out_specs=[ANY] * 4,
            scratch_shapes=[pltpu.VMEM(OUTS[3], F32), pltpu.SemaphoreType.DMA((5,))],
            compiler_params=pltpu.CompilerParams(vmem_limit_bytes=16 * 1024 * 1024),
            name="write",
        )(*mid)
    )


def solution(mesh):
    return jax.shard_map(
        per_device,
        mesh=mesh,
        in_specs=(P("wide", "narrow", None),),
        out_specs=(
            P(None, "wide", "narrow", None),
            P(None, "wide", "narrow", None),
            P(None, "wide", "narrow", None),
            P(None, None, "narrow", None),
        ),
        check_vma=False,
    )
```
